128 devices in a mesh: tile: 8 (over x, core), sweep: 16 (over z, y).
Axes of the slice: x: 4, y: 4, z: 4, core: 2. Of those that a mesh axis runs over, the one named last changes fastest.
Arguments:
- map_tiles: bfloat16 [128, 128, 512], P('tile'), may hold values from -6 to 6
- sweeps: bfloat16 [2, 128, 512, 512], P(None, ('tile', 'sweep')), may hold values from -6 to 6
- cotangents: bfloat16 [2, 128, 2, 512, 512], P(None, ('tile', 'sweep')), may hold values from -1.5 to 1.5
- offsets: int32 [2, 8], replicated, may hold values from 0 to 124
- turn_counts: int32 [2, 128, 2], P(None, ('tile', 'sweep')), may hold values from 0 to 3
Outputs:
- grad_map: float32 [128, 128, 512], P('tile', 'sweep')
- grad_sweeps: float32 [2, 128, 512, 512], P(None, ('tile', 'sweep'))
The draws below stay inside these ranges and needn't reach their ends.
All inputs are finite; a program needn't handle non-finite values.
Results may differ from the reference program's by a relative error of at most 0.013.
Values may be sent and summed in bfloat16 or wider, within the bound.
No kernel may reach another device: no remote copies, remote signals or barrier semaphores. Data moves between devices by JAX's collectives and lax.ppermute only.
A program may use at most 128 MiB of HBM per device.

```python
import math
from functools import partial
import jax
import jax.numpy as jnp
from jax import lax

SIDE = 512
WINDOW_TILES = 4
ROUNDS = 2
TILES_DEV = 16
TILE_ROWS = 128
TILES = 128
BATCH = 128
N_TILE = 8
N_SWEEP = 16


def place_ends(values, key, low, largest):
    spot = [jax.random.randint(jax.random.fold_in(key, axis), (), 0, length) for axis, length in enumerate(values.shape)]
    longest = values.shape.index(max(values.shape))
    next_to = spot[:longest] + [(spot[longest] + 1) % values.shape[longest]] + spot[longest + 1:]
    return values.at[tuple(spot)].set(low).at[tuple(next_to)].set(largest)


def steps_of(key, shape, cuts, smallest, top_value):
    gain, own = 1.0, jax.random.fold_in(key, 6)
    for position, blocks in cuts:
        draws = jnp.exp(jax.random.uniform(jax.random.fold_in(own, position), (blocks,), jnp.float32, smallest / len(cuts), top_value / len(cuts)))
        gain = gain * jnp.repeat(draws, shape[position] // blocks).reshape([-1 if axis == position else 1 for axis in range(len(shape))])
    return gain


def gaussian(own_key, shape, scale, limit, split=(), kind=jnp.bfloat16):
    entries = scale * jax.random.normal(own_key, shape, jnp.float32)
    if split:
        entries = entries * steps_of(own_key, shape, split, -0.22, 0.18)
    return jnp.clip(entries, -limit, limit).astype(kind)


def setup_inputs(seed: int = 0) -> dict:
    arg_keys = jax.random.split(jax.random.key(seed), 6)
    map_tiles = gaussian(arg_keys[0], (TILES, TILE_ROWS, SIDE), 1.0, 6.0, ((0, 8),))
    sweeps = gaussian(arg_keys[1], (ROUNDS, BATCH, SIDE, SIDE), 1.0, 6.0, ((1, 128),))
    cotangents = gaussian(arg_keys[2], (ROUNDS, BATCH, 2, SIDE, SIDE), 0.25, 1.5, ((1, 128),))
    offsets = place_ends(jax.random.randint(arg_keys[3], (ROUNDS, N_TILE), 0, TILES - WINDOW_TILES + 1), jax.random.fold_in(arg_keys[3], 1), 0, TILES - WINDOW_TILES).astype(jnp.int32)
    turn_counts = place_ends(jax.random.randint(arg_keys[4], (ROUNDS, BATCH, 2), 0, 4), jax.random.fold_in(arg_keys[4], 1), 0, 3).astype(jnp.int32)
    return dict(map_tiles=map_tiles, sweeps=sweeps, cotangents=cotangents, offsets=offsets, turn_counts=turn_counts)


def tables(side):
    counter = jnp.arange(side, dtype=jnp.int32)
    product = counter[:, None] * counter[None, :] % side
    angle = product.astype(jnp.float32) * (2.0 * math.pi / side)
    factor = 1.0 / math.sqrt(side)
    return ((jnp.cos(angle) * factor).astype(jnp.bfloat16), (jnp.sin(angle) * factor).astype(jnp.bfloat16))

def columns(row_pass, cosine, sine_table):
    middle = row_pass.shape[1] // 2
    with_cos = jnp.dot(cosine, row_pass, preferred_element_type=jnp.float32)
    with_sin = jnp.dot(sine_table, row_pass, preferred_element_type=jnp.float32)
    real_part = with_cos[:, :middle] + with_sin[:, middle:]
    imag_part = with_cos[:, middle:] - with_sin[:, :middle]
    return jnp.concatenate([real_part, imag_part], 1).astype(jnp.bfloat16)

def forward(field, cosine, sine_table, row_table):
    row_pass = jnp.dot(field, row_table, preferred_element_type=jnp.float32).astype(jnp.bfloat16)
    return columns(row_pass, cosine, sine_table)

def inverse(spectrum, cosine, sine_table, back_table):
    middle = spectrum.shape[1] // 2
    with_cos = jnp.dot(cosine, spectrum, preferred_element_type=jnp.float32)
    with_sin = jnp.dot(sine_table, spectrum, preferred_element_type=jnp.float32)
    mixed = jnp.concatenate([with_cos[:, :middle] - with_sin[:, middle:], with_cos[:, middle:] + with_sin[:, :middle]], 1).astype(jnp.bfloat16)
    return jnp.dot(mixed, back_table, preferred_element_type=jnp.float32)

def rotate(field, quarters):
    return lax.switch(quarters, [partial(jnp.rot90, k=quarter) for quarter in range(4)], field)

def halves(spectrum):
    middle = spectrum.shape[1] // 2
    return (spectrum[:, :middle].astype(jnp.float32), spectrum[:, middle:].astype(jnp.float32))

def local_terms(window_spec, sweep_field, cotangent_pair, quarter_pair, cosine, sine_table, row_table, back_table):
    window_real, window_imag = halves(window_spec)
    total_real = jnp.zeros(window_real.shape, jnp.float32)
    total_imag = jnp.zeros(window_real.shape, jnp.float32)
    gradient = jnp.zeros((window_real.shape[0], window_real.shape[0]), jnp.float32)
    for rotation in range(cotangent_pair.shape[0]):
        rotated = rotate(sweep_field, quarter_pair[rotation])
        sweep_real, sweep_imag = halves(forward(rotated, cosine, sine_table, row_table))
        cot_real, cot_imag = halves(forward(cotangent_pair[rotation], cosine, sine_table, row_table))
        total_real = total_real + (cot_real * sweep_real - cot_imag * sweep_imag)
        total_imag = total_imag + (cot_real * sweep_imag + cot_imag * sweep_real)
        back = jnp.concatenate([cot_real * window_real + cot_imag * window_imag, cot_real * window_imag - cot_imag * window_real], 1).astype(jnp.bfloat16)
        gradient = gradient + rotate(inverse(back, cosine, sine_table, back_table), (4 - quarter_pair[rotation]) % 4)
    map_term = jnp.concatenate([total_real, total_imag], 1).astype(jnp.bfloat16)
    return (map_term, gradient)

def reference(map_tiles, sweeps, cotangents, offsets, turn_counts):
    cosine, sine_table = tables(SIDE)
    row_table = jnp.concatenate([cosine, -sine_table], 1)
    back_table = jnp.concatenate([cosine, -sine_table], 0)
    within = jnp.arange(WINDOW_TILES, dtype=jnp.int32)
    member_ids = jnp.arange(N_SWEEP, dtype=jnp.int32)
    grad_map = jnp.zeros((TILES, TILE_ROWS, SIDE), jnp.float32)
    grad_rounds = []
    for sweep_round in range(ROUNDS):

        def one_group(group_index):
            placed = offsets[sweep_round, group_index] + within
            stored = (placed % N_TILE * TILES_DEV + placed // N_TILE).astype(jnp.int32)
            window = map_tiles[stored].reshape(SIDE, SIDE)
            window_spec = forward(window, cosine, sine_table, row_table)

            def one_member(member):
                batch_index = group_index * N_SWEEP + member
                map_term, gradient = local_terms(window_spec, sweeps[sweep_round, batch_index], cotangents[sweep_round, batch_index], turn_counts[sweep_round, batch_index], cosine, sine_table, row_table, back_table)
                return (inverse(map_term, cosine, sine_table, back_table), gradient)
            window_terms, gradients = lax.map(one_member, member_ids)
            window_grad = lax.optimization_barrier(jnp.sum(window_terms, 0)).reshape(WINDOW_TILES, TILE_ROWS, SIDE)
            return (window_grad, gradients, stored)
        window_grads, gradients, stored = lax.map(one_group, jnp.arange(N_TILE, dtype=jnp.int32))
        grad_map = grad_map.at[stored.reshape(-1)].add(window_grads.reshape(-1, TILE_ROWS, SIDE))
        grad_rounds.append(gradients.reshape(N_TILE * N_SWEEP, SIDE, SIDE))
    return (grad_map, jnp.stack(grad_rounds, 0))
```

```python
from functools import partial
import math

import jax
import jax.numpy as jnp
import ml_dtypes
import numpy as np
from jax import lax
from jax.experimental import pallas as pl
from jax.experimental.pallas import tpu as pltpu
from jax.sharding import PartitionSpec as P

BF = jnp.bfloat16
F32 = jnp.float32
NT = (((1,), (1,)), ((), ()))


def flipped(even, odd, axis):
    return np.flip(even, axis), -np.flip(odd, axis)


def make_tables(side, order):
    half, quarter = side // 2, side // 4
    factor = 1.0 / math.sqrt(side)
    n = np.arange(half)
    alternating = np.where(n % 2 == 0, factor, -factor)

    def cs(n_ids, k_ids):
        angle = (np.outer(n_ids, k_ids) % side) * (2.0 * math.pi / side)
        return np.cos(angle) * factor, np.sin(angle) * factor

    low_even = 2 * np.arange(quarter)
    low_odd = low_even + 1
    all_even = 2 * np.arange(half)
    all_odd = all_even + 1
    c, s = cs(low_even, n)
    s[0] = -alternating
    down_e = np.concatenate([c, -s], 0)
    c, s = cs(low_odd, n)
    down_o = np.concatenate([c, -s], 0)
    across_e = np.concatenate(cs(n, all_even), 1)
    across_o = np.concatenate(cs(n, all_odd), 1)
    c, s = cs(n, low_even)
    s[:, 0] = -0.5 * alternating
    c[:, 0] *= 0.5
    up_e = 2.0 * np.concatenate([c, -s], 1)
    c, s = cs(n, low_odd)
    up_o = 2.0 * np.concatenate([c, -s], 1)

    def back_across(reverse):
        out = []
        for ids, sign in ((all_even, 1.0), (all_odd, -1.0)):
            parts = cs(ids, n)
            if reverse:
                parts = [np.flip(p, 1) * sign for p in parts]
            out.append(np.concatenate(parts, 1))
        return np.stack(out)

    def cast(x):
        return jnp.asarray(np.asarray(x, np.float32).astype(ml_dtypes.bfloat16))

    down = np.stack([np.stack([down_e, down_o]), np.stack(flipped(down_e, down_o, 1))])
    across = np.stack([np.stack([across_e, across_o]), np.stack(flipped(across_e, across_o, 0))])
    back = np.stack([back_across(False), back_across(True)])
    up = np.stack([np.stack([up_e, up_o]), np.stack(flipped(up_e, up_o, 0))])
    up_sent = np.stack([up_e[order], up_o[order]])
    return cast(down), cast(across), cast(back), cast(up), cast(up_sent)


def mm(a, b, dims=(((1,), (0,)), ((), ()))):
    return lax.dot_general(a, b, dims, preferred_element_type=F32)


def fold_columns(product):
    half = product.shape[1] // 2
    left, right = product[:, :half], product[:, half:]
    return (left + right).astype(BF), (left - right).astype(BF)


def row_pass(field, down, flip, plus, minus):
    half = plus.shape[1]
    top, bottom = field
    for parity, folded in ((0, top + bottom), (1, top - bottom)):
        p, m = fold_columns(mm(down[flip, parity], folded))
        plus[parity * half : (parity + 1) * half] = p
        minus[parity * half : (parity + 1) * half] = m


def row_pass_turned(field, down, flip, plus, minus):
    half = plus.shape[1]
    left, right = field[:, :half], field[:, half:]
    for parity, folded in ((0, left + right), (1, left - right)):
        p, m = fold_columns(mm(down[flip, parity], folded, NT))
        plus[parity * half : (parity + 1) * half] = p
        minus[parity * half : (parity + 1) * half] = m


def column_pass(plus, minus, across, flip, store, store_extra):
    half = plus.shape[1]
    quarter = half // 2
    for col, folded in ((0, plus), (1, minus)):
        table = across[flip, col]
        for row in (0, 1):
            both = mm(folded[row * half : (row + 1) * half], table)
            ea, fa = both[:quarter, :half], both[:quarter, half:]
            eb, fb = both[quarter:, :half], both[quarter:, half:]
            if row == 0:
                store_extra(col, eb[:8], -fb[:8])
                first = lax.broadcasted_iota(jnp.int32, eb.shape, 0) == 0
                eb = jnp.where(first, 0.0, eb)
                fb = jnp.where(first, 0.0, fb)
            store(row, col, ea + fb, eb - fa)


def inverse(packed, back, back_flip, up, up_index, middle):
    half = packed.shape[1] // 2
    quarter = half // 2
    for row in (0, 1):
        rows = packed[row * half : (row + 1) * half]
        parts = []
        for col in (0, 1):
            both = mm(rows[:, col * half : (col + 1) * half], back[back_flip, col])
            ea, fa = both[:quarter, :half], both[:quarter, half:]
            eb, fb = both[quarter:, :half], both[quarter:, half:]
            parts.append((ea - fb, eb + fa))
        (re, ie), (ro, io) = parts
        base = row * half
        middle[base : base + quarter, :half] = (re + ro).astype(BF)
        middle[base : base + quarter, half:] = (re - ro).astype(BF)
        middle[base + quarter : base + half, :half] = (ie + io).astype(BF)
        middle[base + quarter : base + half, half:] = (ie - io).astype(BF)
    even = mm(up_index(up, 0), middle[:half])
    odd = mm(up_index(up, 1), middle[half:])
    return even + odd, even - odd


def blocks(half):
    quarter = half // 2
    for row in (0, 1):
        for col in (0, 1):
            real = (slice(row * half, row * half + quarter), slice(col * half, (col + 1) * half))
            imag = (slice(row * half + quarter, (row + 1) * half), real[1])
            yield row, col, real, imag


def merge_row(real, imag, extra_real, extra_imag):
    pad = jnp.zeros((real.shape[0] - 8, real.shape[1]), F32)
    first = lax.broadcasted_iota(jnp.int32, extra_real.shape, 0) == 0
    extra_real = jnp.concatenate([jnp.where(first, extra_real, 0.0), pad], 0)
    extra_imag = jnp.concatenate([jnp.where(first, extra_imag, 0.0), pad], 0)
    return real - extra_imag, imag + extra_real


def map_kernel(
    turns, sweep, cots, down, across, back, up_sent, spec, spec_extra, sent,
    plus, minus, swept, swept_extra, total, total_extra, packed, middle,
):
    q = pl.program_id(0)
    side = sweep.shape[1]
    half = side // 2

    for r in range(cots.shape[1]):
        turn = turns[q, r]
        flip_rows = ((turn == 1) | (turn == 2)).astype(jnp.int32)
        flip_cols = (turn >= 2).astype(jnp.int32)

        @pl.when(turn % 2 == 0)
        def _():
            row_pass((sweep[0, :half], sweep[0, half:]), down, flip_rows, plus, minus)

        @pl.when(turn % 2 == 1)
        def _():
            row_pass_turned(sweep.at[0], down, flip_rows, plus, minus)

        def keep(row, col, real, imag):
            rows = slice(row * (half // 2), (row + 1) * (half // 2))
            swept[0, rows, col * half : (col + 1) * half] = real
            swept[1, rows, col * half : (col + 1) * half] = imag

        def keep_extra(col, real, imag):
            swept_extra[0, :, col * half : (col + 1) * half] = real
            swept_extra[1, :, col * half : (col + 1) * half] = imag

        column_pass(plus, minus, across, flip_cols, keep, keep_extra)
        row_pass((cots[0, r, :half], cots[0, r, half:]), down, 0, plus, minus)

        def meet(row, col, real, imag):
            quarter = half // 2
            base = row * half
            cols = slice(col * half, (col + 1) * half)
            rows = slice(row * quarter, (row + 1) * quarter)
            spec[0, r, base : base + quarter, cols] = real.astype(BF)
            spec[0, r, base + quarter : base + half, cols] = imag.astype(BF)
            sr, si = swept[0, rows, cols], swept[1, rows, cols]
            tr, ti = real * sr - imag * si, real * si + imag * sr
            if r > 0:
                tr, ti = total[0, rows, cols] + tr, total[1, rows, cols] + ti
            if r < cots.shape[1] - 1:
                total[0, rows, cols] = tr
                total[1, rows, cols] = ti
            else:
                if row == 0:
                    tr, ti = merge_row(tr, ti, total_extra[0, :, cols], total_extra[1, :, cols])
                packed[base : base + quarter, cols] = tr.astype(BF)
                packed[base + quarter : base + half, cols] = ti.astype(BF)

        def meet_extra(col, real, imag):
            cols = slice(col * half, (col + 1) * half)
            spec_extra[0, r, 0, :, cols] = real
            spec_extra[0, r, 1, :, cols] = imag
            sr, si = swept_extra[0, :, cols], swept_extra[1, :, cols]
            tr, ti = real * sr - imag * si, real * si + imag * sr
            if r > 0:
                tr, ti = total_extra[0, :, cols] + tr, total_extra[1, :, cols] + ti
            total_extra[0, :, cols] = tr
            total_extra[1, :, cols] = ti

        column_pass(plus, minus, across, 0, meet, meet_extra)

    top, bottom = inverse(packed, back, 0, up_sent, lambda u, parity: u[parity], middle)
    parts = sent.shape[1]
    rows = half // parts
    sent[0, :, :rows] = top.astype(BF).reshape(parts, rows, side)
    sent[0, :, rows:] = bottom.astype(BF).reshape(parts, rows, side)


def sweep_kernel(
    turns, source, tiles, spec, spec_extra, down, across, back, up, out,
    plus, minus, window, window_extra, packed, middle, total,
):
    q = pl.program_id(0)
    side = out.shape[2]
    half = side // 2
    quarter = half // 2

    def tile(k):
        return tiles[source[q, k], 0]

    top = jnp.concatenate([tile(0), tile(1)], 0)
    bottom = jnp.concatenate([tile(2), tile(3)], 0)
    row_pass((top, bottom), down, 0, plus, minus)

    def keep(row, col, real, imag):
        rows = slice(row * quarter, (row + 1) * quarter)
        window[0, rows, col * half : (col + 1) * half] = real
        window[1, rows, col * half : (col + 1) * half] = imag

    def keep_extra(col, real, imag):
        window_extra[0, :, col * half : (col + 1) * half] = real
        window_extra[1, :, col * half : (col + 1) * half] = imag

    column_pass(plus, minus, across, 0, keep, keep_extra)
    total[...] = jnp.zeros_like(total)
    for r in range(spec.shape[1]):
        turn = turns[q, r]
        flip_rows = ((turn == 1) | (turn == 2)).astype(jnp.int32)
        flip_cols = (turn >= 2).astype(jnp.int32)
        for row, col, real, imag in blocks(half):
            rows = slice(row * quarter, (row + 1) * quarter)
            cols = real[1]
            gr, gi = spec[(0, r) + real].astype(F32), spec[(0, r) + imag].astype(F32)
            wr, wi = window[0, rows, cols], window[1, rows, cols]
            br, bi = gr * wr + gi * wi, gr * wi - gi * wr
            if row == 0:
                gr, gi = spec_extra[0, r, 0, :, cols], spec_extra[0, r, 1, :, cols]
                wr, wi = window_extra[0, :, cols], window_extra[1, :, cols]
                br, bi = merge_row(br, bi, gr * wr + gi * wi, gr * wi - gi * wr)
            packed[real] = br.astype(BF)
            packed[imag] = bi.astype(BF)
        top, bottom = inverse(
            packed, back, flip_cols, up, lambda u, parity: u[flip_rows, parity], middle
        )
        total[turn % 2, :half] += top
        total[turn % 2, half:] += bottom
    out[0, 0] = total[0] + total[1].T


def pick_kernel(wanted, tiles, out, sem):
    groups, rounds = out.shape[:2]
    copies = [
        pltpu.make_async_copy(tiles.at[wanted[q, i]], out.at[i, q], sem.at[q, i])
        for i in range(groups)
        for q in range(rounds)
    ]
    for copy in copies:
        copy.start()
    for copy in copies:
        copy.wait()


def spread_kernel(position, own, first, second, third, out):
    rounds = own.shape[0]
    groups, slots = position.shape[1], out.shape[1]
    share = out.shape[2] // rounds
    side = own.shape[2]
    summed = (
        own[...].astype(F32) + first[...].astype(F32) + second[...].astype(F32) + third[...].astype(F32)
    )
    span = own.shape[1] // (slots * share)
    summed = summed.reshape(rounds, span, slots, share, side)
    for i in range(groups):
        parts = []
        for q in range(rounds):
            part = jnp.zeros((slots, share, side), F32)
            for k in range(span):
                part = jnp.where(position[q, i] == k, summed[q, k], part)
            parts.append(part)
        out[i] = jnp.concatenate(parts, 1).astype(BF)


def gather_kernel(wanted, holding, incoming, out):
    rounds, groups = wanted.shape
    share = out.shape[1]
    out[...] = jnp.zeros_like(out)
    for i in range(groups):
        summed = jnp.sum(incoming[i].astype(F32), 0)
        for q in range(rounds):

            @pl.when(holding[q, i] == 1)
            def _():
                out[wanted[q, i]] += summed[q * share : (q + 1) * share]


def full(shape):
    return pl.BlockSpec(shape, lambda *_: (0,) * len(shape))


SMEM = pl.BlockSpec(memory_space=pltpu.SMEM)
VMEM = pl.BlockSpec(memory_space=pltpu.VMEM)
ANY = pl.BlockSpec(memory_space=pl.ANY)
PARAMS = pltpu.CompilerParams(vmem_limit_bytes=50 * 1024 * 1024)


def shards(map_tiles, sweeps, cotangents, offsets, turn_counts):
    groups = lax.axis_size("tile")
    members = lax.axis_size("sweep")
    own_group = lax.axis_index("tile")
    own_member = lax.axis_index("sweep")
    tile_rows, side = map_tiles.shape[1:]
    rounds = sweeps.shape[0]
    hypotheses = cotangents.shape[2]
    half = side // 2
    span = side // tile_rows
    share = tile_rows // members
    near = 4
    far = members // near
    turns = turn_counts[:, 0]
    sweeps = sweeps[:, 0]
    cotangents = cotangents[:, 0]

    order = (
        np.arange(half).reshape(span // 2, far, near, share).transpose(2, 0, 1, 3).reshape(-1)
    )
    down, across, back, up, up_sent = make_tables(side, order)

    peers = jnp.arange(groups, dtype=jnp.int32)
    step = (own_group - offsets) % groups
    holding = (step < span).astype(jnp.int32)
    wanted = jnp.where(step < span, (offsets + step) // groups, 0).astype(jnp.int32)
    own_start = lax.dynamic_slice_in_dim(offsets, own_group, 1, 1)
    source = ((own_start + jnp.arange(span, dtype=jnp.int32)) % groups).astype(jnp.int32)
    position = ((peers[None] - own_start) % groups).astype(jnp.int32)

    outgoing = pl.pallas_call(
        pick_kernel,
        out_shape=jax.ShapeDtypeStruct((groups, rounds, tile_rows, side), BF),
        in_specs=[SMEM, ANY],
        out_specs=ANY,
        scratch_shapes=[pltpu.SemaphoreType.DMA((rounds, groups))],
        name="pick",
    )(wanted, map_tiles)
    incoming = lax.all_to_all(outgoing, "tile", split_axis=0, concat_axis=0, tiled=True)

    unit = 2 * side**3
    spec, spec_extra, sent = pl.pallas_call(
        map_kernel,
        grid=(rounds,),
        out_shape=[
            jax.ShapeDtypeStruct((rounds, hypotheses, side, side), BF),
            jax.ShapeDtypeStruct((rounds, hypotheses, 2, 8, side), F32),
            jax.ShapeDtypeStruct((rounds, near, side // near, side), BF),
        ],
        in_specs=[
            SMEM,
            pl.BlockSpec((1, side, side), lambda q: (q, 0, 0)),
            pl.BlockSpec((1, hypotheses, side, side), lambda q: (q, 0, 0, 0)),
            full(down.shape),
            full(across.shape),
            full(back.shape),
            full(up_sent.shape),
        ],
        out_specs=[
            pl.BlockSpec((1, hypotheses, side, side), lambda q: (q, 0, 0, 0)),
            pl.BlockSpec((1, hypotheses, 2, 8, side), lambda q: (q, 0, 0, 0, 0)),
            pl.BlockSpec((1, near, side // near, side), lambda q: (q, 0, 0, 0)),
        ],
        scratch_shapes=[
            pltpu.VMEM((side, half), BF),
            pltpu.VMEM((side, half), BF),
            pltpu.VMEM((2, half, side), F32),
            pltpu.VMEM((2, 8, side), F32),
            pltpu.VMEM((2, half, side), F32),
            pltpu.VMEM((2, 8, side), F32),
            pltpu.VMEM((side, side), BF),
            pltpu.VMEM((side, side), BF),
        ],
        compiler_params=PARAMS,
        cost_estimate=pl.CostEstimate(
            flops=int(8 * rounds * unit), bytes_accessed=8 * 1024 * 1024, transcendentals=0
        ),
        name="map_terms",
    )(turns, sweeps, cotangents, down, across, back, up_sent)

    own_near = own_member % near
    received = [lax.dynamic_index_in_dim(sent, own_near, 1, keepdims=False)]
    for shift in range(1, near):
        target = (own_near + shift) % near
        block = lax.dynamic_index_in_dim(sent, target, 1, keepdims=False)
        pairs = [(m, m // near * near + (m + shift) % near) for m in range(members)]
        received.append(lax.ppermute(block, "sweep", pairs))

    spread = pl.pallas_call(
        spread_kernel,
        out_shape=jax.ShapeDtypeStruct((groups, far, rounds * share, side), BF),
        in_specs=[SMEM] + [VMEM] * near,
        out_specs=VMEM,
        compiler_params=PARAMS,
        name="spread",
    )(position, *received)
    index_groups = [
        [t * members + f * near + y for t in range(groups) for f in range(far)] for y in range(near)
    ]
    spread = spread.reshape(groups * far, rounds * share, side)
    landed = lax.all_to_all(
        spread,
        ("tile", "sweep"),
        split_axis=0,
        concat_axis=0,
        tiled=True,
        axis_index_groups=index_groups,
    )
    grad_map = pl.pallas_call(
        gather_kernel,
        out_shape=jax.ShapeDtypeStruct((map_tiles.shape[0], share, side), F32),
        in_specs=[SMEM, SMEM, VMEM],
        out_specs=VMEM,
        compiler_params=PARAMS,
        name="gather",
    )(wanted, holding, landed.reshape(groups, far, rounds * share, side))

    grad_sweeps = pl.pallas_call(
        sweep_kernel,
        grid=(rounds,),
        out_shape=jax.ShapeDtypeStruct((rounds, 1, side, side), F32),
        in_specs=[
            SMEM,
            SMEM,
            pl.BlockSpec((groups, 1, tile_rows, side), lambda q: (0, q, 0, 0)),
            pl.BlockSpec((1, hypotheses, side, side), lambda q: (q, 0, 0, 0)),
            pl.BlockSpec((1, hypotheses, 2, 8, side), lambda q: (q, 0, 0, 0, 0)),
            full(down.shape),
            full(across.shape),
            full(back.shape),
            full(up.shape),
        ],
        out_specs=pl.BlockSpec((1, 1, side, side), lambda q: (q, 0, 0, 0)),
        scratch_shapes=[
            pltpu.VMEM((side, half), BF),
            pltpu.VMEM((side, half), BF),
            pltpu.VMEM((2, half, side), F32),
            pltpu.VMEM((2, 8, side), F32),
            pltpu.VMEM((side, side), BF),
            pltpu.VMEM((side, side), BF),
            pltpu.VMEM((2, side, side), F32),
        ],
        compiler_params=PARAMS,
        cost_estimate=pl.CostEstimate(
            flops=int(5 * rounds * unit), bytes_accessed=8 * 1024 * 1024, transcendentals=0
        ),
        name="sweep_terms",
    )(turns, source, incoming, spec, spec_extra, down, across, back, up)
    return grad_map, grad_sweeps


def solution(mesh):
    in_specs = (
        P("tile", None, None),
        P(None, ("tile", "sweep"), None, None),
        P(None, ("tile", "sweep"), None, None, None),
        P(),
        P(None, ("tile", "sweep"), None),
    )
    out_specs = (P("tile", "sweep", None), P(None, ("tile", "sweep"), None, None))
    return jax.shard_map(shards, mesh=mesh, in_specs=in_specs, out_specs=out_specs, check_vma=False)
```

```python
from functools import partial
import math

import jax
import jax.numpy as jnp
import ml_dtypes
import numpy as np
from jax import lax
from jax.experimental import pallas as pl
from jax.experimental.pallas import tpu as pltpu
from jax.sharding import PartitionSpec as P

BF = jnp.bfloat16
F32 = jnp.float32
NT = (((1,), (1,)), ((), ()))


def flipped(even, odd, axis):
    return np.flip(even, axis), -np.flip(odd, axis)


def make_tables(side, order, near):
    half, quarter = side // 2, side // 4
    factor = 1.0 / math.sqrt(side)
    n = np.arange(half)
    alternating = np.where(n % 2 == 0, factor, -factor)

    def cs(n_ids, k_ids):
        angle = (np.outer(n_ids, k_ids) % side) * (2.0 * math.pi / side)
        return np.cos(angle) * factor, np.sin(angle) * factor

    low_even = 2 * np.arange(quarter)
    low_odd = low_even + 1
    all_even = 2 * np.arange(half)
    all_odd = all_even + 1
    c, s = cs(low_even, n)
    s[0] = -alternating
    down_e = np.concatenate([c, -s], 0)
    c, s = cs(low_odd, n)
    down_o = np.concatenate([c, -s], 0)
    across_e = np.concatenate(cs(n, all_even), 1)
    across_o = np.concatenate(cs(n, all_odd), 1)
    c, s = cs(n, low_even)
    s[:, 0] = -0.5 * alternating
    c[:, 0] *= 0.5
    up_e = 2.0 * np.concatenate([c, -s], 1)
    c, s = cs(n, low_odd)
    up_o = 2.0 * np.concatenate([c, -s], 1)

    def back_across(reverse):
        out = []
        for ids, sign in ((all_even, 1.0), (all_odd, -1.0)):
            parts = cs(ids, n)
            if reverse:
                parts = [np.flip(p, 1) * sign for p in parts]
            out.append(np.concatenate(parts, 1))
        return np.stack(out)

    def cast(x):
        return jnp.asarray(np.asarray(x, np.float32).astype(ml_dtypes.bfloat16))

    down = np.stack([np.stack([down_e, down_o]), np.stack(flipped(down_e, down_o, 1))])
    across = np.stack([np.stack([across_e, across_o]), np.stack(flipped(across_e, across_o, 0))])
    back = np.stack([back_across(False), back_across(True)])
    up = np.stack([np.stack([up_e, up_o]), np.stack(flipped(up_e, up_o, 0))])
    up_sent = np.stack([up_e[order], up_o[order]]).reshape(2, near, half // near, half)
    return cast(down), cast(across), cast(back), cast(up), cast(up_sent)


def mm(a, b, dims=(((1,), (0,)), ((), ()))):
    return lax.dot_general(a, b, dims, preferred_element_type=F32)


def fold_columns(product):
    half = product.shape[1] // 2
    left, right = product[:, :half], product[:, half:]
    return (left + right).astype(BF), (left - right).astype(BF)


def row_pass(field, down, flip, plus, minus):
    half = plus.shape[1]
    top, bottom = field
    for parity, folded in ((0, top + bottom), (1, top - bottom)):
        p, m = fold_columns(mm(down[flip, parity], folded))
        plus[parity * half : (parity + 1) * half] = p
        minus[parity * half : (parity + 1) * half] = m


def row_pass_turned(field, down, flip, plus, minus):
    half = plus.shape[1]
    left, right = field[:, :half], field[:, half:]
    for parity, folded in ((0, left + right), (1, left - right)):
        p, m = fold_columns(mm(down[flip, parity], folded, NT))
        plus[parity * half : (parity + 1) * half] = p
        minus[parity * half : (parity + 1) * half] = m


def column_pass(plus, minus, across, flip, store, store_extra):
    half = plus.shape[1]
    quarter = half // 2
    for col, folded in ((0, plus), (1, minus)):
        table = across[flip, col]
        for row in (0, 1):
            both = mm(folded[row * half : (row + 1) * half], table)
            ea, fa = both[:quarter, :half], both[:quarter, half:]
            eb, fb = both[quarter:, :half], both[quarter:, half:]
            if row == 0:
                store_extra(col, eb[:8], -fb[:8])
                first = lax.broadcasted_iota(jnp.int32, eb.shape, 0) == 0
                eb = jnp.where(first, 0.0, eb)
                fb = jnp.where(first, 0.0, fb)
            store(row, col, ea + fb, eb - fa)


def inverse(packed, back, back_flip, up, up_index, middle):
    half = packed.shape[1] // 2
    quarter = half // 2
    for row in (0, 1):
        rows = packed[row * half : (row + 1) * half]
        parts = []
        for col in (0, 1):
            both = mm(rows[:, col * half : (col + 1) * half], back[back_flip, col])
            ea, fa = both[:quarter, :half], both[:quarter, half:]
            eb, fb = both[quarter:, :half], both[quarter:, half:]
            parts.append((ea - fb, eb + fa))
        (re, ie), (ro, io) = parts
        base = row * half
        middle[base : base + quarter, :half] = (re + ro).astype(BF)
        middle[base : base + quarter, half:] = (re - ro).astype(BF)
        middle[base + quarter : base + half, :half] = (ie + io).astype(BF)
        middle[base + quarter : base + half, half:] = (ie - io).astype(BF)
    even = mm(up_index(up, 0), middle[:half])
    odd = mm(up_index(up, 1), middle[half:])
    return even + odd, even - odd


def blocks(half):
    quarter = half // 2
    for row in (0, 1):
        for col in (0, 1):
            real = (slice(row * half, row * half + quarter), slice(col * half, (col + 1) * half))
            imag = (slice(row * half + quarter, (row + 1) * half), real[1])
            yield row, col, real, imag


def merge_row(real, imag, extra_real, extra_imag):
    pad = jnp.zeros((real.shape[0] - 8, real.shape[1]), F32)
    first = lax.broadcasted_iota(jnp.int32, extra_real.shape, 0) == 0
    extra_real = jnp.concatenate([jnp.where(first, extra_real, 0.0), pad], 0)
    extra_imag = jnp.concatenate([jnp.where(first, extra_imag, 0.0), pad], 0)
    return real - extra_imag, imag + extra_real


def members_of(near):
    member = lax.axis_index("sweep")
    return member // near, member % near


def map_kernel(
    turns, sweep, cots, down, across, back, up_sent, spec, spec_extra, *rest
):
    q = pl.program_id(0)
    near = up_sent.shape[1]
    sent, rest = rest[:near], rest[near:]
    plus, minus, swept, swept_extra, total, total_extra, packed, middle = rest
    side = sweep.shape[1]
    half = side // 2
    quarter = half // 2
    hypotheses = cots.shape[1]

    for r in range(hypotheses):
        turn = turns[q, 0, r]
        flip_rows = ((turn == 1) | (turn == 2)).astype(jnp.int32)
        flip_cols = (turn >= 2).astype(jnp.int32)

        @pl.when(turn % 2 == 0)
        def _():
            row_pass((sweep[0, :half], sweep[0, half:]), down, flip_rows, plus, minus)

        @pl.when(turn % 2 == 1)
        def _():
            row_pass_turned(sweep.at[0], down, flip_rows, plus, minus)

        def keep(row, col, real, imag):
            rows = slice(row * quarter, (row + 1) * quarter)
            swept[0, rows, col * half : (col + 1) * half] = real
            swept[1, rows, col * half : (col + 1) * half] = imag

        def keep_extra(col, real, imag):
            swept_extra[0, :, col * half : (col + 1) * half] = real
            swept_extra[1, :, col * half : (col + 1) * half] = imag

        column_pass(plus, minus, across, flip_cols, keep, keep_extra)
        row_pass((cots[0, r, :half], cots[0, r, half:]), down, 0, plus, minus)

        def meet(row, col, real, imag):
            base = row * half
            cols = slice(col * half, (col + 1) * half)
            rows = slice(row * quarter, (row + 1) * quarter)
            spec[0, r, base : base + quarter, cols] = real.astype(BF)
            spec[0, r, base + quarter : base + half, cols] = imag.astype(BF)
            sr, si = swept[0, rows, cols], swept[1, rows, cols]
            tr, ti = real * sr - imag * si, real * si + imag * sr
            if r > 0:
                tr, ti = total[0, rows, cols] + tr, total[1, rows, cols] + ti
            if r < hypotheses - 1:
                total[0, rows, cols] = tr
                total[1, rows, cols] = ti
            else:
                if row == 0:
                    tr, ti = merge_row(tr, ti, total_extra[0, :, cols], total_extra[1, :, cols])
                packed[base : base + quarter, cols] = tr.astype(BF)
                packed[base + quarter : base + half, cols] = ti.astype(BF)

        def meet_extra(col, real, imag):
            cols = slice(col * half, (col + 1) * half)
            spec_extra[0, r, 0, :, cols] = real
            spec_extra[0, r, 1, :, cols] = imag
            sr, si = swept_extra[0, :, cols], swept_extra[1, :, cols]
            tr, ti = real * sr - imag * si, real * si + imag * sr
            if r > 0:
                tr, ti = total_extra[0, :, cols] + tr, total_extra[1, :, cols] + ti
            total_extra[0, :, cols] = tr
            total_extra[1, :, cols] = ti

        column_pass(plus, minus, across, 0, meet, meet_extra)

    _, own = members_of(near)
    ahead = [(own + shift) % near for shift in range(near)]

    def up_index(table, parity):
        return jnp.concatenate([table[parity, y] for y in ahead], 0)

    top, bottom = inverse(packed, back, 0, up_sent, up_index, middle)
    top, bottom = top.astype(BF), bottom.astype(BF)
    rows = half // near
    for shift in range(near):
        sent[shift][0, :rows] = top[shift * rows : (shift + 1) * rows]
        sent[shift][0, rows:] = bottom[shift * rows : (shift + 1) * rows]


def sweep_kernel(
    offsets, turns, tiles, spec, spec_extra, down, across, back, up, out,
    plus, minus, window, window_extra, packed, middle, total,
):
    q = pl.program_id(0)
    side = out.shape[2]
    half = side // 2
    quarter = half // 2
    groups, _, tile_rows, _ = tiles.shape
    start = offsets[q, lax.axis_index("tile")]

    def tile(k):
        return tiles[(start + k) % groups, 0]

    top = jnp.concatenate([tile(k) for k in range(half // tile_rows)], 0)
    bottom = jnp.concatenate([tile(k + half // tile_rows) for k in range(half // tile_rows)], 0)
    row_pass((top, bottom), down, 0, plus, minus)

    def keep(row, col, real, imag):
        rows = slice(row * quarter, (row + 1) * quarter)
        window[0, rows, col * half : (col + 1) * half] = real
        window[1, rows, col * half : (col + 1) * half] = imag

    def keep_extra(col, real, imag):
        window_extra[0, :, col * half : (col + 1) * half] = real
        window_extra[1, :, col * half : (col + 1) * half] = imag

    column_pass(plus, minus, across, 0, keep, keep_extra)
    total[...] = jnp.zeros_like(total)
    for r in range(spec.shape[1]):
        turn = turns[q, 0, r]
        flip_rows = ((turn == 1) | (turn == 2)).astype(jnp.int32)
        flip_cols = (turn >= 2).astype(jnp.int32)
        for row, col, real, imag in blocks(half):
            rows = slice(row * quarter, (row + 1) * quarter)
            cols = real[1]
            gr, gi = spec[(0, r) + real].astype(F32), spec[(0, r) + imag].astype(F32)
            wr, wi = window[0, rows, cols], window[1, rows, cols]
            br, bi = gr * wr + gi * wi, gr * wi - gi * wr
            if row == 0:
                gr, gi = spec_extra[0, r, 0, :, cols], spec_extra[0, r, 1, :, cols]
                wr, wi = window_extra[0, :, cols], window_extra[1, :, cols]
                br, bi = merge_row(br, bi, gr * wr + gi * wi, gr * wi - gi * wr)
            packed[real] = br.astype(BF)
            packed[imag] = bi.astype(BF)
        top, bottom = inverse(
            packed, back, flip_cols, up, lambda u, parity: u[flip_rows, parity], middle
        )
        total[turn % 2, :half] += top
        total[turn % 2, half:] += bottom
    out[0, 0] = total[0] + total[1].T


def held_tile(offsets, q, i, span):
    groups = lax.axis_size("tile")
    step = (lax.axis_index("tile") - offsets[q, i] + groups * (groups * span)) % groups
    held = step < span
    return held, jnp.where(held, (offsets[q, i] + step) // groups, 0)


def pick_kernel(offsets, tiles, out, held_tiles, in_sems, out_sems):
    groups, rounds, tile_rows, side = out.shape
    places = [(i, q) for i in range(groups) for q in range(rounds)]
    held, moves = [], []
    for i, q in places:
        here, index = held_tile(offsets, q, i, side // tile_rows)
        held.append(here)
        moves.append(
            (
                pltpu.make_async_copy(tiles.at[index], held_tiles.at[i, q], in_sems.at[i, q]),
                pltpu.make_async_copy(held_tiles.at[i, q], out.at[i, q], out_sems.at[i, q]),
            )
        )
        pl.when(here)(moves[-1][0].start)
    for here, (load, store) in zip(held, moves):

        @pl.when(here)
        def _():
            load.wait()
            store.start()

    for here, (_, store) in zip(held, moves):
        pl.when(here)(store.wait)


def near_kernel(offsets, *refs):
    landed, out, scratch = refs[:-2], refs[-2], refs[-1]
    groups = out.shape[0]
    rounds, span, far, share, side = scratch.shape
    summed = landed[0][...].astype(F32)
    for block in landed[1:]:
        summed += block[...].astype(F32)
    scratch[...] = summed.reshape(rounds, span, far, share, side)
    own = lax.axis_index("tile")
    for i in range(groups):
        parts = []
        for q in range(rounds):
            k = (i - offsets[q, own] + groups * (groups * span)) % groups
            part = scratch[q, jnp.minimum(k, span - 1)]
            parts.append(jnp.where(k < span, part, 0.0))
        out[i] = jnp.concatenate(parts, 1).astype(BF)


def gather_kernel(span, offsets, incoming, out):
    rounds, groups = offsets.shape
    share = out.shape[1]
    out[...] = jnp.zeros_like(out)
    for i in range(groups):
        rows = jnp.sum(incoming[i].astype(F32), 0)
        for q in range(rounds):
            held, index = held_tile(offsets, q, i, span)

            @pl.when(held)
            def _():
                out[index] += rows[q * share : (q + 1) * share]


def full(shape):
    return pl.BlockSpec(shape, lambda *_: (0,) * len(shape))


SMEM = pl.BlockSpec(memory_space=pltpu.SMEM)
VMEM = pl.BlockSpec(memory_space=pltpu.VMEM)
ANY = pl.BlockSpec(memory_space=pl.ANY)
SMALL = pltpu.CompilerParams(vmem_limit_bytes=12 * 1024 * 1024)
LARGE = pltpu.CompilerParams(vmem_limit_bytes=60 * 1024 * 1024)


def shape(dims, dtype):
    return jax.ShapeDtypeStruct(dims, dtype)


def per_round(dims):
    return pl.BlockSpec((1,) + dims, lambda q: (q,) + (0,) * len(dims))


def shards(map_tiles, sweeps, cotangents, offsets, turn_counts):
    groups = lax.axis_size("tile")
    members = lax.axis_size("sweep")
    tile_rows, side = map_tiles.shape[1:]
    rounds = sweeps.shape[0]
    hypotheses = cotangents.shape[2]
    half = side // 2
    span = side // tile_rows
    share = tile_rows // members
    near = 4
    far = members // near
    sweeps = sweeps[:, 0]
    cotangents = cotangents[:, 0]

    order = (
        np.arange(half).reshape(span // 2, far, near, share).transpose(2, 0, 1, 3).reshape(-1)
    )
    down, across, back, up, up_sent = make_tables(side, order, near)

    outgoing = pl.pallas_call(
        pick_kernel,
        out_shape=shape((groups, rounds, tile_rows, side), BF),
        in_specs=[SMEM, ANY],
        out_specs=ANY,
        scratch_shapes=[
            pltpu.VMEM((groups, rounds, tile_rows, side), BF),
            pltpu.SemaphoreType.DMA((groups, rounds)),
            pltpu.SemaphoreType.DMA((groups, rounds)),
        ],
        compiler_params=pltpu.CompilerParams(vmem_limit_bytes=60 * 1024 * 1024),
        name="pick",
    )(offsets, map_tiles)
    incoming = lax.all_to_all(outgoing, "tile", split_axis=0, concat_axis=0, tiled=True)

    unit = 2 * side**3
    spec, spec_extra, *sent = pl.pallas_call(
        map_kernel,
        grid=(rounds,),
        out_shape=[
            shape((rounds, hypotheses, side, side), BF),
            shape((rounds, hypotheses, 2, 8, side), F32),
            *[shape((rounds, side // near, side), BF)] * near,
        ],
        in_specs=[
            SMEM,
            per_round((side, side)),
            per_round((hypotheses, side, side)),
            full(down.shape),
            full(across.shape),
            full(back.shape),
            full(up_sent.shape),
        ],
        out_specs=[
            per_round((hypotheses, side, side)),
            per_round((hypotheses, 2, 8, side)),
            *[per_round((side // near, side))] * near,
        ],
        scratch_shapes=[
            pltpu.VMEM((side, half), BF),
            pltpu.VMEM((side, half), BF),
            pltpu.VMEM((2, half, side), F32),
            pltpu.VMEM((2, 8, side), F32),
            pltpu.VMEM((2, half, side), F32),
            pltpu.VMEM((2, 8, side), F32),
            pltpu.VMEM((side, side), BF),
            pltpu.VMEM((side, side), BF),
        ],
        compiler_params=LARGE,
        cost_estimate=pl.CostEstimate(
            flops=int(8 * rounds * unit), bytes_accessed=8 * 1024 * 1024, transcendentals=0
        ),
        name="map_terms",
    )(turn_counts, sweeps, cotangents, down, across, back, up_sent)
    landed = [sent[0]]
    for shift in range(1, near):
        pairs = [(m, m // near * near + (m + shift) % near) for m in range(members)]
        landed.append(lax.ppermute(sent[shift], "sweep", pairs))

    placed = pl.pallas_call(
        near_kernel,
        out_shape=shape((groups, far, rounds * share, side), BF),
        in_specs=[SMEM] + [VMEM] * near,
        out_specs=VMEM,
        scratch_shapes=[pltpu.VMEM((rounds, span, far, share, side), F32)],
        compiler_params=SMALL,
        name="near_sum",
    )(offsets, *landed)
    placed, incoming = lax.optimization_barrier((placed, incoming))
    index_groups = [
        [t * members + f * near + y for t in range(groups) for f in range(far)] for y in range(near)
    ]
    owned = lax.all_to_all(
        placed.reshape(groups * far, rounds * share, side),
        ("tile", "sweep"),
        split_axis=0,
        concat_axis=0,
        tiled=True,
        axis_index_groups=index_groups,
    )
    grad_map = pl.pallas_call(
        partial(gather_kernel, span),
        out_shape=shape((map_tiles.shape[0], share, side), F32),
        in_specs=[SMEM, VMEM],
        out_specs=VMEM,
        compiler_params=SMALL,
        name="gather",
    )(offsets, owned.reshape(groups, far, rounds * share, side))

    grad_sweeps = pl.pallas_call(
        sweep_kernel,
        grid=(rounds,),
        out_shape=shape((rounds, 1, side, side), F32),
        in_specs=[
            SMEM,
            SMEM,
            pl.BlockSpec((groups, 1, tile_rows, side), lambda q: (0, q, 0, 0)),
            per_round((hypotheses, side, side)),
            per_round((hypotheses, 2, 8, side)),
            full(down.shape),
            full(across.shape),
            full(back.shape),
            full(up.shape),
        ],
        out_specs=per_round((1, side, side)),
        scratch_shapes=[
            pltpu.VMEM((side, half), BF),
            pltpu.VMEM((side, half), BF),
            pltpu.VMEM((2, half, side), F32),
            pltpu.VMEM((2, 8, side), F32),
            pltpu.VMEM((side, side), BF),
            pltpu.VMEM((side, side), BF),
            pltpu.VMEM((2, side, side), F32),
        ],
        compiler_params=LARGE,
        cost_estimate=pl.CostEstimate(
            flops=int(5 * rounds * unit), bytes_accessed=8 * 1024 * 1024, transcendentals=0
        ),
        name="sweep_terms",
    )(offsets, turn_counts, incoming, spec, spec_extra, down, across, back, up)
    return grad_map, grad_sweeps


def solution(mesh):
    in_specs = (
        P("tile", None, None),
        P(None, ("tile", "sweep"), None, None),
        P(None, ("tile", "sweep"), None, None, None),
        P(),
        P(None, ("tile", "sweep"), None),
    )
    out_specs = (P("tile", "sweep", None), P(None, ("tile", "sweep"), None, None))
    return jax.shard_map(shards, mesh=mesh, in_specs=in_specs, out_specs=out_specs, check_vma=False)
```

```python
from functools import partial
import math

import jax
import jax.numpy as jnp
import ml_dtypes
import numpy as np
from jax import lax
from jax.experimental import pallas as pl
from jax.experimental.pallas import tpu as pltpu
from jax.sharding import PartitionSpec as P

BF = jnp.bfloat16
F32 = jnp.float32
NT = (((1,), (1,)), ((), ()))


def flipped(even, odd, axis):
    return np.flip(even, axis), -np.flip(odd, axis)


def make_tables(side, order, near):
    half, quarter = side // 2, side // 4
    factor = 1.0 / math.sqrt(side)
    n = np.arange(half)
    alternating = np.where(n % 2 == 0, factor, -factor)

    def cs(n_ids, k_ids):
        angle = (np.outer(n_ids, k_ids) % side) * (2.0 * math.pi / side)
        return np.cos(angle) * factor, np.sin(angle) * factor

    low_even = 2 * np.arange(quarter)
    low_odd = low_even + 1
    all_even = 2 * np.arange(half)
    all_odd = all_even + 1
    c, s = cs(low_even, n)
    s[0] = -alternating
    down_e = np.concatenate([c, -s], 0)
    c, s = cs(low_odd, n)
    down_o = np.concatenate([c, -s], 0)
    across_e = np.concatenate(cs(n, all_even), 1)
    across_o = np.concatenate(cs(n, all_odd), 1)
    c, s = cs(n, low_even)
    s[:, 0] = -0.5 * alternating
    c[:, 0] *= 0.5
    up_e = 2.0 * np.concatenate([c, -s], 1)
    c, s = cs(n, low_odd)
    up_o = 2.0 * np.concatenate([c, -s], 1)

    def back_across(reverse):
        out = []
        for ids, sign in ((all_even, 1.0), (all_odd, -1.0)):
            parts = cs(ids, n)
            if reverse:
                parts = [np.flip(p, 1) * sign for p in parts]
            out.append(np.concatenate(parts, 1))
        return np.stack(out)

    def cast(x):
        return jnp.asarray(np.asarray(x, np.float32).astype(ml_dtypes.bfloat16))

    down = np.stack([np.stack([down_e, down_o]), np.stack(flipped(down_e, down_o, 1))])
    across = np.stack([np.stack([across_e, across_o]), np.stack(flipped(across_e, across_o, 0))])
    back = np.stack([back_across(False), back_across(True)])
    up = np.stack([np.stack([up_e, up_o]), np.stack(flipped(up_e, up_o, 0))])
    up_sent = np.stack([up_e[order], up_o[order]]).reshape(2, near, half // near, half)
    return cast(down), cast(across), cast(back), cast(up), cast(up_sent)


def mm(a, b, dims=(((1,), (0,)), ((), ()))):
    return lax.dot_general(a, b, dims, preferred_element_type=F32)


def fold_columns(product):
    half = product.shape[1] // 2
    left, right = product[:, :half], product[:, half:]
    return (left + right).astype(BF), (left - right).astype(BF)


def row_pass(field, down, flip, plus, minus):
    half = plus.shape[1]
    top, bottom = field
    for parity, folded in ((0, top + bottom), (1, top - bottom)):
        p, m = fold_columns(mm(down[flip, parity], folded))
        plus[parity * half : (parity + 1) * half] = p
        minus[parity * half : (parity + 1) * half] = m


def row_pass_turned(field, down, flip, plus, minus):
    half = plus.shape[1]
    left, right = field[:, :half], field[:, half:]
    for parity, folded in ((0, left + right), (1, left - right)):
        p, m = fold_columns(mm(down[flip, parity], folded, NT))
        plus[parity * half : (parity + 1) * half] = p
        minus[parity * half : (parity + 1) * half] = m


def column_pass(plus, minus, across, flip, store, store_extra):
    half = plus.shape[1]
    quarter = half // 2
    for col, folded in ((0, plus), (1, minus)):
        table = across[flip, col]
        for row in (0, 1):
            both = mm(folded[row * half : (row + 1) * half], table)
            ea, fa = both[:quarter, :half], both[:quarter, half:]
            eb, fb = both[quarter:, :half], both[quarter:, half:]
            if row == 0:
                store_extra(col, eb[:8], -fb[:8])
                first = lax.broadcasted_iota(jnp.int32, eb.shape, 0) == 0
                eb = jnp.where(first, 0.0, eb)
                fb = jnp.where(first, 0.0, fb)
            store(row, col, ea + fb, eb - fa)


def inverse(packed, back, back_flip, up, up_index, middle):
    half = packed.shape[1] // 2
    quarter = half // 2
    for row in (0, 1):
        rows = packed[row * half : (row + 1) * half]
        parts = []
        for col in (0, 1):
            both = mm(rows[:, col * half : (col + 1) * half], back[back_flip, col])
            ea, fa = both[:quarter, :half], both[:quarter, half:]
            eb, fb = both[quarter:, :half], both[quarter:, half:]
            parts.append((ea - fb, eb + fa))
        (re, ie), (ro, io) = parts
        base = row * half
        middle[base : base + quarter, :half] = (re + ro).astype(BF)
        middle[base : base + quarter, half:] = (re - ro).astype(BF)
        middle[base + quarter : base + half, :half] = (ie + io).astype(BF)
        middle[base + quarter : base + half, half:] = (ie - io).astype(BF)
    even = mm(up_index(up, 0), middle[:half])
    odd = mm(up_index(up, 1), middle[half:])
    return even + odd, even - odd


def blocks(half):
    quarter = half // 2
    for row in (0, 1):
        for col in (0, 1):
            real = (slice(row * half, row * half + quarter), slice(col * half, (col + 1) * half))
            imag = (slice(row * half + quarter, (row + 1) * half), real[1])
            yield row, col, real, imag


def merge_row(real, imag, extra_real, extra_imag):
    pad = jnp.zeros((real.shape[0] - 8, real.shape[1]), F32)
    first = lax.broadcasted_iota(jnp.int32, extra_real.shape, 0) == 0
    extra_real = jnp.concatenate([jnp.where(first, extra_real, 0.0), pad], 0)
    extra_imag = jnp.concatenate([jnp.where(first, extra_imag, 0.0), pad], 0)
    return real - extra_imag, imag + extra_real


def members_of(near):
    member = lax.axis_index("sweep")
    return member // near, member % near


def map_kernel(
    offsets, turns, tiles, sweep, cots, down, across, back, up_sent,
    outgoing, spec, spec_extra, *rest
):
    near = up_sent.shape[1]
    sent, rest = rest[:near], rest[near:]
    plus, minus, swept, swept_extra, total, total_extra, packed, middle = rest[:8]
    staged, in_sems, out_sems = rest[8:]
    q = pl.program_id(0)
    rounds = outgoing.shape[1]
    side = sweep.shape[1]
    half = side // 2
    quarter = half // 2
    moves = pick(offsets, tiles, outgoing, staged, in_sems, out_sems, side // tiles.shape[1])

    @pl.when(q == 0)
    def _():
        for here, load, _ in moves:
            pl.when(here)(load.start)

    hypotheses = cots.shape[1]

    flips = []
    for r in range(hypotheses):
        turn = turns[q, 0, r]
        flip_rows = ((turn == 1) | (turn == 2)).astype(jnp.int32)
        flips.append((turn >= 2).astype(jnp.int32))

        @pl.when(turn % 2 == 0)
        def _():
            row_pass((sweep[0, :half], sweep[0, half:]), down, flip_rows, plus.at[r], minus.at[r])

        @pl.when(turn % 2 == 1)
        def _():
            row_pass_turned(sweep.at[0], down, flip_rows, plus.at[r], minus.at[r])

    for r in range(hypotheses):
        cot = hypotheses + r

        def keep(row, col, real, imag):
            rows = slice(row * quarter, (row + 1) * quarter)
            swept[r, 0, rows, col * half : (col + 1) * half] = real
            swept[r, 1, rows, col * half : (col + 1) * half] = imag

        def keep_extra(col, real, imag):
            swept_extra[r, 0, :, col * half : (col + 1) * half] = real
            swept_extra[r, 1, :, col * half : (col + 1) * half] = imag

        column_pass(plus.at[r], minus.at[r], across, flips[r], keep, keep_extra)
        row_pass((cots[0, r, :half], cots[0, r, half:]), down, 0, plus.at[cot], minus.at[cot])

        def meet(row, col, real, imag):
            base = row * half
            cols = slice(col * half, (col + 1) * half)
            rows = slice(row * quarter, (row + 1) * quarter)
            spec[0, r, base : base + quarter, cols] = real.astype(BF)
            spec[0, r, base + quarter : base + half, cols] = imag.astype(BF)
            sr, si = swept[r, 0, rows, cols], swept[r, 1, rows, cols]
            tr, ti = real * sr - imag * si, real * si + imag * sr
            if r > 0:
                tr, ti = total[0, rows, cols] + tr, total[1, rows, cols] + ti
            if r < hypotheses - 1:
                total[0, rows, cols] = tr
                total[1, rows, cols] = ti
            else:
                if row == 0:
                    tr, ti = merge_row(tr, ti, total_extra[0, :, cols], total_extra[1, :, cols])
                packed[base : base + quarter, cols] = tr.astype(BF)
                packed[base + quarter : base + half, cols] = ti.astype(BF)

        def meet_extra(col, real, imag):
            cols = slice(col * half, (col + 1) * half)
            spec_extra[0, r, 0, :, cols] = real
            spec_extra[0, r, 1, :, cols] = imag
            sr, si = swept_extra[r, 0, :, cols], swept_extra[r, 1, :, cols]
            tr, ti = real * sr - imag * si, real * si + imag * sr
            if r > 0:
                tr, ti = total_extra[0, :, cols] + tr, total_extra[1, :, cols] + ti
            total_extra[0, :, cols] = tr
            total_extra[1, :, cols] = ti

        column_pass(plus.at[cot], minus.at[cot], across, 0, meet, meet_extra)

    _, own = members_of(near)
    ahead = [(own + shift) % near for shift in range(near)]

    def up_index(table, parity):
        return jnp.concatenate([table[parity, y] for y in ahead], 0)

    top, bottom = inverse(packed, back, 0, up_sent, up_index, middle)
    top, bottom = top.astype(BF), bottom.astype(BF)
    rows = half // near
    for shift in range(near):
        sent[shift][0, :rows] = top[shift * rows : (shift + 1) * rows]
        sent[shift][0, rows:] = bottom[shift * rows : (shift + 1) * rows]

    @pl.when(q == 0)
    def _():
        for here, load, store in moves:

            @pl.when(here)
            def _():
                load.wait()
                store.start()

    @pl.when(q == rounds - 1)
    def _():
        for here, _, store in moves:
            pl.when(here)(store.wait)


def sweep_kernel(
    offsets, turns, kept, others, spec, spec_extra, down, across, back, up, out,
    field, plus, minus, window, window_extra, packed, middle, total,
):
    q = pl.program_id(0)
    side = out.shape[2]
    half = side // 2
    quarter = half // 2
    span, rows_kept = kept.shape[1:3]
    parts = others.shape[0] + 1
    own_part, _ = members_of(near=others.shape[0] + 1)
    for shift in range(parts):
        source = kept if shift == 0 else others.at[shift - 1]
        part = (own_part - shift + parts) % parts
        for k in range(span):
            at = pl.multiple_of((parts * k + part) * rows_kept, rows_kept)
            field[pl.ds(at, rows_kept), :] = source[0, k]
    row_pass((field[:half], field[half:]), down, 0, plus, minus)

    def keep(row, col, real, imag):
        rows = slice(row * quarter, (row + 1) * quarter)
        window[0, rows, col * half : (col + 1) * half] = real
        window[1, rows, col * half : (col + 1) * half] = imag

    def keep_extra(col, real, imag):
        window_extra[0, :, col * half : (col + 1) * half] = real
        window_extra[1, :, col * half : (col + 1) * half] = imag

    column_pass(plus, minus, across, 0, keep, keep_extra)
    total[...] = jnp.zeros_like(total)

    def one_rotation(r, carry):
        turn = turns[q, 0, r]
        flip_rows = ((turn == 1) | (turn == 2)).astype(jnp.int32)
        flip_cols = (turn >= 2).astype(jnp.int32)
        for row, col, real, imag in blocks(half):
            rows, cols = slice(row * quarter, (row + 1) * quarter), real[1]
            gr, gi = spec[(0, r) + real].astype(F32), spec[(0, r) + imag].astype(F32)
            wr, wi = window[0, rows, cols], window[1, rows, cols]
            br, bi = gr * wr + gi * wi, gr * wi - gi * wr
            if row == 0:
                gr, gi = spec_extra[0, r, 0, :, cols], spec_extra[0, r, 1, :, cols]
                wr, wi = window_extra[0, :, cols], window_extra[1, :, cols]
                br, bi = merge_row(br, bi, gr * wr + gi * wi, gr * wi - gi * wr)
            packed[real] = br.astype(BF)
            packed[imag] = bi.astype(BF)
        top, bottom = inverse(
            packed, back, flip_cols, up, lambda u, parity: u[flip_rows, parity], middle
        )
        total[turn % 2, :half] += top
        total[turn % 2, half:] += bottom
        return carry

    lax.fori_loop(0, spec.shape[1], one_rotation, 0)
    out[0, 0] = total[0] + total[1].T


def held_tile(offsets, q, i, span):
    groups = lax.axis_size("tile")
    step = (lax.axis_index("tile") - offsets[q, i] + groups * (groups * span)) % groups
    held = step < span
    return held, jnp.where(held, (offsets[q, i] + step) // groups, 0)


def pick(offsets, tiles, out, staged, in_sems, out_sems, span):
    groups, rounds, rows, _ = out.shape
    part, _ = members_of(tiles.shape[1] // rows)
    first = pl.multiple_of(part * rows, rows)
    moves = []
    for i in range(groups):
        for q in range(rounds):
            here, index = held_tile(offsets, q, i, span)
            load = pltpu.make_async_copy(
                tiles.at[index, pl.ds(first, rows)], staged.at[i, q], in_sems.at[i, q]
            )
            store = pltpu.make_async_copy(staged.at[i, q], out.at[i, q], out_sems.at[i, q])
            moves.append((here, load, store))
    return moves


def choose_kernel(offsets, incoming, out, token):
    rounds, span = out.shape[:2]
    own = lax.axis_index("tile")
    for q in range(rounds):
        for k in range(span):
            out[q, k] = incoming[(offsets[q, own] + k) % incoming.shape[0], q]
    token[...] = jnp.zeros_like(token)


def near_kernel(offsets, token, *refs):
    del token
    landed, out, scratch = refs[:-2], refs[-2], refs[-1]
    groups = out.shape[0]
    rounds, span, far, share, side = scratch.shape
    summed = landed[0][...].astype(F32)
    for block in landed[1:]:
        summed += block[...].astype(F32)
    scratch[...] = summed.reshape(rounds, span, far, share, side)
    own = lax.axis_index("tile")
    for i in range(groups):
        parts = []
        for q in range(rounds):
            k = (i - offsets[q, own] + groups * (groups * span)) % groups
            part = scratch[q, jnp.minimum(k, span - 1)]
            parts.append(jnp.where(k < span, part, 0.0))
        out[i] = jnp.concatenate(parts, 1).astype(BF)


def gather_kernel(span, offsets, incoming, out):
    rounds, groups = offsets.shape
    share = out.shape[1]
    out[...] = jnp.zeros_like(out)
    for i in range(groups):
        rows = jnp.sum(incoming[i].astype(F32), 0)
        for q in range(rounds):
            held, index = held_tile(offsets, q, i, span)

            @pl.when(held)
            def _():
                out[index] += rows[q * share : (q + 1) * share]


def full(shape):
    return pl.BlockSpec(shape, lambda *_: (0,) * len(shape))


SMEM = pl.BlockSpec(memory_space=pltpu.SMEM)
VMEM = pl.BlockSpec(memory_space=pltpu.VMEM)
ANY = pl.BlockSpec(memory_space=pl.ANY)
SMALL = pltpu.CompilerParams(vmem_limit_bytes=12 * 1024 * 1024)
LARGE = pltpu.CompilerParams(vmem_limit_bytes=60 * 1024 * 1024)


def shape(dims, dtype):
    return jax.ShapeDtypeStruct(dims, dtype)


def per_round(dims):
    return pl.BlockSpec((1,) + dims, lambda q: (q,) + (0,) * len(dims))


def shards(map_tiles, sweeps, cotangents, offsets, turn_counts):
    groups = lax.axis_size("tile")
    members = lax.axis_size("sweep")
    tile_rows, side = map_tiles.shape[1:]
    rounds = sweeps.shape[0]
    hypotheses = cotangents.shape[2]
    half = side // 2
    span = side // tile_rows
    share = tile_rows // members
    near = 4
    far = members // near
    sweeps = sweeps[:, 0]
    cotangents = cotangents[:, 0]

    order = (
        np.arange(half).reshape(span // 2, far, near, share).transpose(2, 0, 1, 3).reshape(-1)
    )
    down, across, back, up, up_sent = make_tables(side, order, near)

    part_rows = tile_rows // far
    unit = 2 * side**3
    outgoing, spec, spec_extra, *sent = pl.pallas_call(
        map_kernel,
        grid=(rounds,),
        out_shape=[
            shape((groups, rounds, part_rows, side), BF),
            shape((rounds, hypotheses, side, side), BF),
            shape((rounds, hypotheses, 2, 8, side), F32),
            *[shape((rounds, side // near, side), BF)] * near,
        ],
        in_specs=[
            SMEM,
            SMEM,
            ANY,
            per_round((side, side)),
            per_round((hypotheses, side, side)),
            full(down.shape),
            full(across.shape),
            full((1,) + back.shape[1:]),
            full(up_sent.shape),
        ],
        out_specs=[
            ANY,
            per_round((hypotheses, side, side)),
            per_round((hypotheses, 2, 8, side)),
            *[per_round((side // near, side))] * near,
        ],
        scratch_shapes=[
            pltpu.VMEM((2 * hypotheses, side, half), BF),
            pltpu.VMEM((2 * hypotheses, side, half), BF),
            pltpu.VMEM((hypotheses, 2, half, side), F32),
            pltpu.VMEM((hypotheses, 2, 8, side), F32),
            pltpu.VMEM((2, half, side), F32),
            pltpu.VMEM((2, 8, side), F32),
            pltpu.VMEM((side, side), BF),
            pltpu.VMEM((side, side), BF),
            pltpu.VMEM((groups, rounds, part_rows, side), BF),
            pltpu.SemaphoreType.DMA((groups, rounds)),
            pltpu.SemaphoreType.DMA((groups, rounds)),
        ],
        compiler_params=LARGE,
        cost_estimate=pl.CostEstimate(
            flops=int(8 * rounds * unit), bytes_accessed=8 * 1024 * 1024, transcendentals=0
        ),
        name="map_terms",
    )(offsets, turn_counts, map_tiles, sweeps, cotangents, down, across, back, up_sent)
    incoming = lax.all_to_all(outgoing, "tile", split_axis=0, concat_axis=0, tiled=True)
    kept, token = pl.pallas_call(
        choose_kernel,
        out_shape=[shape((rounds, span, part_rows, side), BF), shape((8, 128), F32)],
        in_specs=[SMEM, VMEM],
        out_specs=[VMEM] * 2,
        compiler_params=SMALL,
        name="choose",
    )(offsets, incoming)
    others = jnp.stack(
        [
            lax.ppermute(kept, "sweep", [(m, (m + shift * near) % members) for m in range(members)])
            for shift in range(1, far)
        ]
    )
    landed = [sent[0]]
    for shift in range(1, near):
        pairs = [(m, m // near * near + (m + shift) % near) for m in range(members)]
        landed.append(lax.ppermute(sent[shift], "sweep", pairs))

    placed = pl.pallas_call(
        near_kernel,
        out_shape=shape((groups, far, rounds * share, side), BF),
        in_specs=[SMEM, VMEM] + [VMEM] * near,
        out_specs=VMEM,
        scratch_shapes=[pltpu.VMEM((rounds, span, far, share, side), F32)],
        compiler_params=SMALL,
        name="near_sum",
    )(offsets, token, *landed)
    index_groups = [
        [t * members + f * near + y for t in range(groups) for f in range(far)] for y in range(near)
    ]
    owned = lax.all_to_all(
        placed.reshape(groups * far, rounds * share, side),
        ("tile", "sweep"),
        split_axis=0,
        concat_axis=0,
        tiled=True,
        axis_index_groups=index_groups,
    )
    grad_map = pl.pallas_call(
        partial(gather_kernel, span),
        out_shape=shape((map_tiles.shape[0], share, side), F32),
        in_specs=[SMEM, VMEM],
        out_specs=VMEM,
        compiler_params=SMALL,
        name="gather",
    )(offsets, owned.reshape(groups, far, rounds * share, side))

    grad_sweeps = pl.pallas_call(
        sweep_kernel,
        grid=(rounds,),
        out_shape=shape((rounds, 1, side, side), F32),
        in_specs=[
            SMEM,
            SMEM,
            per_round((span, part_rows, side)),
            pl.BlockSpec((far - 1, 1, span, part_rows, side), lambda q: (0, q, 0, 0, 0)),
            per_round((hypotheses, side, side)),
            per_round((hypotheses, 2, 8, side)),
            full(down.shape),
            full(across.shape),
            full(back.shape),
            full(up.shape),
        ],
        out_specs=per_round((1, side, side)),
        scratch_shapes=[
            pltpu.VMEM((side, side), BF),
            pltpu.VMEM((side, half), BF),
            pltpu.VMEM((side, half), BF),
            pltpu.VMEM((2, half, side), F32),
            pltpu.VMEM((2, 8, side), F32),
            pltpu.VMEM((side, side), BF),
            pltpu.VMEM((side, side), BF),
            pltpu.VMEM((2, side, side), F32),
        ],
        compiler_params=LARGE,
        cost_estimate=pl.CostEstimate(
            flops=int(5 * rounds * unit), bytes_accessed=8 * 1024 * 1024, transcendentals=0
        ),
        name="sweep_terms",
    )(offsets, turn_counts, kept, others, spec, spec_extra, down, across, back, up)
    return grad_map, grad_sweeps


def solution(mesh):
    in_specs = (
        P("tile", None, None),
        P(None, ("tile", "sweep"), None, None),
        P(None, ("tile", "sweep"), None, None, None),
        P(),
        P(None, ("tile", "sweep"), None),
    )
    out_specs = (P("tile", "sweep", None), P(None, ("tile", "sweep"), None, None))
    return jax.shard_map(shards, mesh=mesh, in_specs=in_specs, out_specs=out_specs, check_vma=False)
```

```python
from functools import partial
import math

import jax
import jax.numpy as jnp
import ml_dtypes
import numpy as np
from jax import lax
from jax.experimental import pallas as pl
from jax.experimental.pallas import tpu as pltpu
from jax.sharding import PartitionSpec as P

BF = jnp.bfloat16
F32 = jnp.float32
NT = (((1,), (1,)), ((), ()))


def flipped(even, odd, axis):
    return np.flip(even, axis), -np.flip(odd, axis)


def make_tables(side, order, near):
    half, quarter = side // 2, side // 4
    factor = 1.0 / math.sqrt(side)
    n = np.arange(half)
    alternating = np.where(n % 2 == 0, factor, -factor)

    def cs(n_ids, k_ids):
        angle = (np.outer(n_ids, k_ids) % side) * (2.0 * math.pi / side)
        return np.cos(angle) * factor, np.sin(angle) * factor

    low_even = 2 * np.arange(quarter)
    low_odd = low_even + 1
    all_even = 2 * np.arange(half)
    all_odd = all_even + 1
    c, s = cs(low_even, n)
    s[0] = -alternating
    down_e = np.concatenate([c, -s], 0)
    c, s = cs(low_odd, n)
    down_o = np.concatenate([c, -s], 0)
    across_e = np.concatenate(cs(n, all_even), 1)
    across_o = np.concatenate(cs(n, all_odd), 1)
    c, s = cs(n, low_even)
    s[:, 0] = -0.5 * alternating
    c[:, 0] *= 0.5
    up_e = 2.0 * np.concatenate([c, -s], 1)
    c, s = cs(n, low_odd)
    up_o = 2.0 * np.concatenate([c, -s], 1)

    def back_across(reverse):
        out = []
        for ids, sign in ((all_even, 1.0), (all_odd, -1.0)):
            parts = cs(ids, n)
            if reverse:
                parts = [np.flip(p, 1) * sign for p in parts]
            out.append(np.concatenate(parts, 1))
        return np.stack(out)

    def cast(x):
        return jnp.asarray(np.asarray(x, np.float32).astype(ml_dtypes.bfloat16))

    down = np.stack([np.stack([down_e, down_o]), np.stack(flipped(down_e, down_o, 1))])
    across = np.stack([np.stack([across_e, across_o]), np.stack(flipped(across_e, across_o, 0))])
    back = np.stack([back_across(False), back_across(True)])
    up = np.stack([np.stack([up_e, up_o]), np.stack(flipped(up_e, up_o, 0))])
    up_sent = np.stack([up_e[order], up_o[order]]).reshape(2, near, half // near, half)
    return cast(down), cast(across), cast(back), cast(up), cast(up_sent)


def mm(a, b, dims=(((1,), (0,)), ((), ()))):
    return lax.dot_general(a, b, dims, preferred_element_type=F32)


def fold_columns(product):
    half = product.shape[1] // 2
    left, right = product[:, :half], product[:, half:]
    return (left + right).astype(BF), (left - right).astype(BF)


def row_pass(field, down, flip, plus, minus):
    half = plus.shape[1]
    top, bottom = field
    for parity, folded in ((0, top + bottom), (1, top - bottom)):
        p, m = fold_columns(mm(down[flip, parity], folded))
        plus[parity * half : (parity + 1) * half] = p
        minus[parity * half : (parity + 1) * half] = m


def row_pass_turned(field, down, flip, plus, minus):
    half = plus.shape[1]
    left, right = field[:, :half], field[:, half:]
    for parity, folded in ((0, left + right), (1, left - right)):
        p, m = fold_columns(mm(down[flip, parity], folded, NT))
        plus[parity * half : (parity + 1) * half] = p
        minus[parity * half : (parity + 1) * half] = m


def column_pass(plus, minus, across, flip, store, store_extra):
    half = plus.shape[1]
    quarter = half // 2
    for col, folded in ((0, plus), (1, minus)):
        table = across[flip, col]
        for row in (0, 1):
            both = mm(folded[row * half : (row + 1) * half], table)
            ea, fa = both[:quarter, :half], both[:quarter, half:]
            eb, fb = both[quarter:, :half], both[quarter:, half:]
            if row == 0:
                store_extra(col, eb[:8], -fb[:8])
                first = lax.broadcasted_iota(jnp.int32, eb.shape, 0) == 0
                eb = jnp.where(first, 0.0, eb)
                fb = jnp.where(first, 0.0, fb)
            store(row, col, ea + fb, eb - fa)


def inverse(packed, back, back_flip, up, up_index, middle):
    half = packed.shape[1] // 2
    quarter = half // 2
    for row in (0, 1):
        rows = packed[row * half : (row + 1) * half]
        parts = []
        for col in (0, 1):
            both = mm(rows[:, col * half : (col + 1) * half], back[back_flip, col])
            ea, fa = both[:quarter, :half], both[:quarter, half:]
            eb, fb = both[quarter:, :half], both[quarter:, half:]
            parts.append((ea - fb, eb + fa))
        (re, ie), (ro, io) = parts
        base = row * half
        middle[base : base + quarter, :half] = (re + ro).astype(BF)
        middle[base : base + quarter, half:] = (re - ro).astype(BF)
        middle[base + quarter : base + half, :half] = (ie + io).astype(BF)
        middle[base + quarter : base + half, half:] = (ie - io).astype(BF)
    even = mm(up_index(up, 0), middle[:half])
    odd = mm(up_index(up, 1), middle[half:])
    return even + odd, even - odd


def blocks(half):
    quarter = half // 2
    for row in (0, 1):
        for col in (0, 1):
            real = (slice(row * half, row * half + quarter), slice(col * half, (col + 1) * half))
            imag = (slice(row * half + quarter, (row + 1) * half), real[1])
            yield row, col, real, imag


def merge_row(real, imag, extra_real, extra_imag):
    pad = jnp.zeros((real.shape[0] - 8, real.shape[1]), F32)
    first = lax.broadcasted_iota(jnp.int32, extra_real.shape, 0) == 0
    extra_real = jnp.concatenate([jnp.where(first, extra_real, 0.0), pad], 0)
    extra_imag = jnp.concatenate([jnp.where(first, extra_imag, 0.0), pad], 0)
    return real - extra_imag, imag + extra_real


def members_of(near):
    member = lax.axis_index("sweep")
    return member // near, member % near


def map_kernel(
    offsets, turns, tiles, sweep, cots, down, across, back, up_sent,
    outgoing, spec, spec_extra, *rest
):
    near = up_sent.shape[1]
    sent, rest = rest[:near], rest[near:]
    plus, minus, swept, swept_extra, total, total_extra, packed, middle = rest[:8]
    staged, in_sems, out_sems = rest[8:]
    q = pl.program_id(0)
    rounds = outgoing.shape[1]
    side = sweep.shape[1]
    half = side // 2
    quarter = half // 2
    moves = pick(offsets, tiles, outgoing, staged, in_sems, out_sems, side // tiles.shape[1])

    @pl.when(q == 0)
    def _():
        for here, load, _ in moves:
            pl.when(here)(load.start)

    hypotheses = cots.shape[1]

    flips = []
    for r in range(hypotheses):
        turn = turns[q, 0, r]
        flip_rows = ((turn == 1) | (turn == 2)).astype(jnp.int32)
        flips.append((turn >= 2).astype(jnp.int32))

        @pl.when(turn % 2 == 0)
        def _():
            row_pass((sweep[0, :half], sweep[0, half:]), down, flip_rows, plus.at[r], minus.at[r])

        @pl.when(turn % 2 == 1)
        def _():
            row_pass_turned(sweep.at[0], down, flip_rows, plus.at[r], minus.at[r])

    for r in range(hypotheses):
        cot = hypotheses + r

        def keep(row, col, real, imag):
            rows = slice(row * quarter, (row + 1) * quarter)
            swept[r, 0, rows, col * half : (col + 1) * half] = real
            swept[r, 1, rows, col * half : (col + 1) * half] = imag

        def keep_extra(col, real, imag):
            swept_extra[r, 0, :, col * half : (col + 1) * half] = real
            swept_extra[r, 1, :, col * half : (col + 1) * half] = imag

        column_pass(plus.at[r], minus.at[r], across, flips[r], keep, keep_extra)
        row_pass((cots[0, r, :half], cots[0, r, half:]), down, 0, plus.at[cot], minus.at[cot])

        def meet(row, col, real, imag):
            base = row * half
            cols = slice(col * half, (col + 1) * half)
            rows = slice(row * quarter, (row + 1) * quarter)
            spec[0, r, base : base + quarter, cols] = real.astype(BF)
            spec[0, r, base + quarter : base + half, cols] = imag.astype(BF)
            sr, si = swept[r, 0, rows, cols], swept[r, 1, rows, cols]
            tr, ti = real * sr - imag * si, real * si + imag * sr
            if r > 0:
                tr, ti = total[0, rows, cols] + tr, total[1, rows, cols] + ti
            if r < hypotheses - 1:
                total[0, rows, cols] = tr
                total[1, rows, cols] = ti
            else:
                if row == 0:
                    tr, ti = merge_row(tr, ti, total_extra[0, :, cols], total_extra[1, :, cols])
                packed[base : base + quarter, cols] = tr.astype(BF)
                packed[base + quarter : base + half, cols] = ti.astype(BF)

        def meet_extra(col, real, imag):
            cols = slice(col * half, (col + 1) * half)
            spec_extra[0, r, 0, :, cols] = real
            spec_extra[0, r, 1, :, cols] = imag
            sr, si = swept_extra[r, 0, :, cols], swept_extra[r, 1, :, cols]
            tr, ti = real * sr - imag * si, real * si + imag * sr
            if r > 0:
                tr, ti = total_extra[0, :, cols] + tr, total_extra[1, :, cols] + ti
            total_extra[0, :, cols] = tr
            total_extra[1, :, cols] = ti

        column_pass(plus.at[cot], minus.at[cot], across, 0, meet, meet_extra)

    _, own = members_of(near)
    ahead = [(own + shift) % near for shift in range(near)]

    def up_index(table, parity):
        return jnp.concatenate([table[parity, y] for y in ahead], 0)

    top, bottom = inverse(packed, back, 0, up_sent, up_index, middle)
    top, bottom = top.astype(BF), bottom.astype(BF)
    rows = half // near
    for shift in range(near):
        sent[shift][0, :rows] = top[shift * rows : (shift + 1) * rows]
        sent[shift][0, rows:] = bottom[shift * rows : (shift + 1) * rows]

    @pl.when(q == 0)
    def _():
        for here, load, store in moves:

            @pl.when(here)
            def _():
                load.wait()
                store.start()

    @pl.when(q == rounds - 1)
    def _():
        for here, _, store in moves:
            pl.when(here)(store.wait)


def sweep_kernel(parts, offsets, turns, *refs):
    quarters, refs = refs[:parts], refs[parts:]
    spec, spec_extra, down, across, back, up, out = refs[:7]
    field, plus, minus, window, window_extra, packed, middle, total = refs[7:]
    q = pl.program_id(0)
    side = out.shape[2]
    half = side // 2
    quarter = half // 2
    span, rows_kept = quarters[0].shape[1:3]
    own_part, _ = members_of(parts)
    for shift in range(parts):
        part = (own_part - shift + parts) % parts
        for k in range(span):
            at = pl.multiple_of((parts * k + part) * rows_kept, rows_kept)
            field[pl.ds(at, rows_kept), :] = quarters[shift][0, k]
    row_pass((field[:half], field[half:]), down, 0, plus, minus)

    def keep(row, col, real, imag):
        rows = slice(row * quarter, (row + 1) * quarter)
        window[0, rows, col * half : (col + 1) * half] = real
        window[1, rows, col * half : (col + 1) * half] = imag

    def keep_extra(col, real, imag):
        window_extra[0, :, col * half : (col + 1) * half] = real
        window_extra[1, :, col * half : (col + 1) * half] = imag

    column_pass(plus, minus, across, 0, keep, keep_extra)
    total[...] = jnp.zeros_like(total)

    for r in range(spec.shape[1]):
        turn = turns[q, 0, r]
        flip_rows = ((turn == 1) | (turn == 2)).astype(jnp.int32)
        flip_cols = (turn >= 2).astype(jnp.int32)
        for row, col, real, imag in blocks(half):
            rows, cols = slice(row * quarter, (row + 1) * quarter), real[1]
            gr, gi = spec[(0, r) + real].astype(F32), spec[(0, r) + imag].astype(F32)
            wr, wi = window[0, rows, cols], window[1, rows, cols]
            br, bi = gr * wr + gi * wi, gr * wi - gi * wr
            if row == 0:
                gr, gi = spec_extra[0, r, 0, :, cols], spec_extra[0, r, 1, :, cols]
                wr, wi = window_extra[0, :, cols], window_extra[1, :, cols]
                br, bi = merge_row(br, bi, gr * wr + gi * wi, gr * wi - gi * wr)
            packed[(r,) + real] = br.astype(BF)
            packed[(r,) + imag] = bi.astype(BF)
        top, bottom = inverse(
            packed.at[r], back, flip_cols, up, lambda u, parity: u[flip_rows, parity], middle.at[r]
        )
        total[turn % 2, :half] += top
        total[turn % 2, half:] += bottom
    out[0, 0] = total[0] + total[1].T


def held_tile(offsets, q, i, span):
    groups = lax.axis_size("tile")
    step = (lax.axis_index("tile") - offsets[q, i] + groups * (groups * span)) % groups
    held = step < span
    return held, jnp.where(held, (offsets[q, i] + step) // groups, 0)


def pick(offsets, tiles, out, staged, in_sems, out_sems, span):
    groups, rounds, rows, _ = out.shape
    part, _ = members_of(tiles.shape[1] // rows)
    first = pl.multiple_of(part * rows, rows)
    moves = []
    for i in range(groups):
        for q in range(rounds):
            here, index = held_tile(offsets, q, i, span)
            load = pltpu.make_async_copy(
                tiles.at[index, pl.ds(first, rows)], staged.at[i, q], in_sems.at[i, q]
            )
            store = pltpu.make_async_copy(staged.at[i, q], out.at[i, q], out_sems.at[i, q])
            moves.append((here, load, store))
    return moves


def choose_kernel(offsets, incoming, out, token):
    rounds, span = out.shape[:2]
    own = lax.axis_index("tile")
    for q in range(rounds):
        for k in range(span):
            out[q, k] = incoming[(offsets[q, own] + k) % incoming.shape[0], q]
    token[...] = jnp.zeros_like(token)


def near_kernel(offsets, token, *refs):
    del token
    landed, out, scratch = refs[:-2], refs[-2], refs[-1]
    groups = out.shape[0]
    rounds, span, far, share, side = scratch.shape
    summed = landed[0][...].astype(F32)
    for block in landed[1:]:
        summed += block[...].astype(F32)
    scratch[...] = summed.reshape(rounds, span, far, share, side)
    own = lax.axis_index("tile")
    for i in range(groups):
        parts = []
        for q in range(rounds):
            k = (i - offsets[q, own] + groups * (groups * span)) % groups
            part = scratch[q, jnp.minimum(k, span - 1)]
            parts.append(jnp.where(k < span, part, 0.0))
        out[i] = jnp.concatenate(parts, 1).astype(BF)


def gather_kernel(span, offsets, incoming, out):
    rounds, groups = offsets.shape
    share = out.shape[1]
    out[...] = jnp.zeros_like(out)
    for i in range(groups):
        rows = jnp.sum(incoming[i].astype(F32), 0)
        for q in range(rounds):
            held, index = held_tile(offsets, q, i, span)
            out[index] += jnp.where(held, rows[q * share : (q + 1) * share], 0.0)


def full(shape):
    return pl.BlockSpec(shape, lambda *_: (0,) * len(shape))


SMEM = pl.BlockSpec(memory_space=pltpu.SMEM)
VMEM = pl.BlockSpec(memory_space=pltpu.VMEM)
ANY = pl.BlockSpec(memory_space=pl.ANY)
SMALL = pltpu.CompilerParams(vmem_limit_bytes=12 * 1024 * 1024)
LARGE = pltpu.CompilerParams(vmem_limit_bytes=60 * 1024 * 1024)


def shape(dims, dtype):
    return jax.ShapeDtypeStruct(dims, dtype)


def per_round(dims):
    return pl.BlockSpec((1,) + dims, lambda q: (q,) + (0,) * len(dims))


def shards(map_tiles, sweeps, cotangents, offsets, turn_counts):
    groups = lax.axis_size("tile")
    members = lax.axis_size("sweep")
    tile_rows, side = map_tiles.shape[1:]
    rounds = sweeps.shape[0]
    hypotheses = cotangents.shape[2]
    half = side // 2
    span = side // tile_rows
    share = tile_rows // members
    near = 4
    far = members // near
    sweeps = sweeps[:, 0]
    cotangents = cotangents[:, 0]

    order = (
        np.arange(half).reshape(span // 2, far, near, share).transpose(2, 0, 1, 3).reshape(-1)
    )
    down, across, back, up, up_sent = make_tables(side, order, near)

    part_rows = tile_rows // far
    unit = 2 * side**3
    outgoing, spec, spec_extra, *sent = pl.pallas_call(
        map_kernel,
        grid=(rounds,),
        out_shape=[
            shape((groups, rounds, part_rows, side), BF),
            shape((rounds, hypotheses, side, side), BF),
            shape((rounds, hypotheses, 2, 8, side), F32),
            *[shape((rounds, side // near, side), BF)] * near,
        ],
        in_specs=[
            SMEM,
            SMEM,
            ANY,
            per_round((side, side)),
            per_round((hypotheses, side, side)),
            full(down.shape),
            full(across.shape),
            full((1,) + back.shape[1:]),
            full(up_sent.shape),
        ],
        out_specs=[
            ANY,
            per_round((hypotheses, side, side)),
            per_round((hypotheses, 2, 8, side)),
            *[per_round((side // near, side))] * near,
        ],
        scratch_shapes=[
            pltpu.VMEM((2 * hypotheses, side, half), BF),
            pltpu.VMEM((2 * hypotheses, side, half), BF),
            pltpu.VMEM((hypotheses, 2, half, side), F32),
            pltpu.VMEM((hypotheses, 2, 8, side), F32),
            pltpu.VMEM((2, half, side), F32),
            pltpu.VMEM((2, 8, side), F32),
            pltpu.VMEM((side, side), BF),
            pltpu.VMEM((side, side), BF),
            pltpu.VMEM((groups, rounds, part_rows, side), BF),
            pltpu.SemaphoreType.DMA((groups, rounds)),
            pltpu.SemaphoreType.DMA((groups, rounds)),
        ],
        compiler_params=LARGE,
        cost_estimate=pl.CostEstimate(
            flops=int(8 * rounds * unit), bytes_accessed=8 * 1024 * 1024, transcendentals=0
        ),
        name="map_terms",
    )(offsets, turn_counts, map_tiles, sweeps, cotangents, down, across, back, up_sent)
    incoming = lax.all_to_all(outgoing, "tile", split_axis=0, concat_axis=0, tiled=True)
    kept, token = pl.pallas_call(
        choose_kernel,
        out_shape=[shape((rounds, span, part_rows, side), BF), shape((8, 128), F32)],
        in_specs=[SMEM, VMEM],
        out_specs=[VMEM] * 2,
        compiler_params=SMALL,
        name="choose",
    )(offsets, incoming)
    quarters = [kept] + [
        lax.ppermute(kept, "sweep", [(m, (m + shift * near) % members) for m in range(members)])
        for shift in range(1, far)
    ]
    landed = [sent[0]]
    for shift in range(1, near):
        pairs = [(m, m // near * near + (m + shift) % near) for m in range(members)]
        landed.append(lax.ppermute(sent[shift], "sweep", pairs))

    placed = pl.pallas_call(
        near_kernel,
        out_shape=shape((groups, far, rounds * share, side), BF),
        in_specs=[SMEM, VMEM] + [VMEM] * near,
        out_specs=VMEM,
        scratch_shapes=[pltpu.VMEM((rounds, span, far, share, side), F32)],
        compiler_params=SMALL,
        name="near_sum",
    )(offsets, token, *landed)
    index_groups = [
        [t * members + f * near + y for t in range(groups) for f in range(far)] for y in range(near)
    ]
    owned = lax.all_to_all(
        placed.reshape(groups * far, rounds * share, side),
        ("tile", "sweep"),
        split_axis=0,
        concat_axis=0,
        tiled=True,
        axis_index_groups=index_groups,
    )
    grad_map = pl.pallas_call(
        partial(gather_kernel, span),
        out_shape=shape((map_tiles.shape[0], share, side), F32),
        in_specs=[SMEM, VMEM],
        out_specs=VMEM,
        compiler_params=SMALL,
        name="gather",
    )(offsets, owned.reshape(groups, far, rounds * share, side))

    grad_sweeps = pl.pallas_call(
        partial(sweep_kernel, far),
        grid=(rounds,),
        out_shape=shape((rounds, 1, side, side), F32),
        in_specs=[
            SMEM,
            SMEM,
            *[per_round((span, part_rows, side))] * far,
            per_round((hypotheses, side, side)),
            per_round((hypotheses, 2, 8, side)),
            full((1,) + down.shape[1:]),
            full((1,) + across.shape[1:]),
            full(back.shape),
            full(up.shape),
        ],
        out_specs=per_round((1, side, side)),
        scratch_shapes=[
            pltpu.VMEM((side, side), BF),
            pltpu.VMEM((side, half), BF),
            pltpu.VMEM((side, half), BF),
            pltpu.VMEM((2, half, side), F32),
            pltpu.VMEM((2, 8, side), F32),
            pltpu.VMEM((hypotheses, side, side), BF),
            pltpu.VMEM((hypotheses, side, side), BF),
            pltpu.VMEM((2, side, side), F32),
        ],
        compiler_params=LARGE,
        cost_estimate=pl.CostEstimate(
            flops=int(5 * rounds * unit), bytes_accessed=8 * 1024 * 1024, transcendentals=0
        ),
        name="sweep_terms",
    )(offsets, turn_counts, *quarters, spec, spec_extra, down, across, back, up)
    return grad_map, grad_sweeps


def solution(mesh):
    in_specs = (
        P("tile", None, None),
        P(None, ("tile", "sweep"), None, None),
        P(None, ("tile", "sweep"), None, None, None),
        P(),
        P(None, ("tile", "sweep"), None),
    )
    out_specs = (P("tile", "sweep", None), P(None, ("tile", "sweep"), None, None))
    return jax.shard_map(shards, mesh=mesh, in_specs=in_specs, out_specs=out_specs, check_vma=False)
```

```python
from functools import partial
import math

import jax
import jax.numpy as jnp
import ml_dtypes
import numpy as np
from jax import lax
from jax.experimental import pallas as pl
from jax.experimental.pallas import tpu as pltpu
from jax.sharding import PartitionSpec as P

BF = jnp.bfloat16
F32 = jnp.float32
NT = (((1,), (1,)), ((), ()))


def flipped(even, odd, axis):
    return np.flip(even, axis), -np.flip(odd, axis)


def make_tables(side, order, near):
    half, quarter = side // 2, side // 4
    factor = 1.0 / math.sqrt(side)
    n = np.arange(half)
    alternating = np.where(n % 2 == 0, factor, -factor)

    def cs(n_ids, k_ids):
        angle = (np.outer(n_ids, k_ids) % side) * (2.0 * math.pi / side)
        return np.cos(angle) * factor, np.sin(angle) * factor

    low_even = 2 * np.arange(quarter)
    low_odd = low_even + 1
    all_even = 2 * np.arange(half)
    all_odd = all_even + 1
    c, s = cs(low_even, n)
    s[0] = -alternating
    down_e = np.concatenate([c, -s], 0)
    c, s = cs(low_odd, n)
    down_o = np.concatenate([c, -s], 0)
    across_e = np.concatenate(cs(n, all_even), 1)
    across_o = np.concatenate(cs(n, all_odd), 1)
    c, s = cs(n, low_even)
    s[:, 0] = -0.5 * alternating
    c[:, 0] *= 0.5
    up_e = 2.0 * np.concatenate([c, -s], 1)
    c, s = cs(n, low_odd)
    up_o = 2.0 * np.concatenate([c, -s], 1)

    def back_across(reverse):
        out = []
        for ids, sign in ((all_even, 1.0), (all_odd, -1.0)):
            parts = cs(ids, n)
            if reverse:
                parts = [np.flip(p, 1) * sign for p in parts]
            out.append(np.concatenate(parts, 1))
        return np.stack(out)

    def cast(x):
        return jnp.asarray(np.asarray(x, np.float32).astype(ml_dtypes.bfloat16))

    down = np.stack([np.stack([down_e, down_o]), np.stack(flipped(down_e, down_o, 1))])
    across = np.stack([np.stack([across_e, across_o]), np.stack(flipped(across_e, across_o, 0))])
    back = np.stack([back_across(False), back_across(True)])
    up = np.stack([np.stack([up_e, up_o]), np.stack(flipped(up_e, up_o, 0))])
    up_sent = np.stack([up_e[order], up_o[order]]).reshape(2, near, half // near, half)
    return cast(down), cast(across), cast(back), cast(up), cast(up_sent)


def mm(a, b, dims=(((1,), (0,)), ((), ()))):
    return lax.dot_general(a, b, dims, preferred_element_type=F32)


def fold_columns(product):
    half = product.shape[1] // 2
    left, right = product[:, :half], product[:, half:]
    return (left + right).astype(BF), (left - right).astype(BF)


def row_pass(field, down, flip, plus, minus):
    half = plus.shape[1]
    top, bottom = field
    for parity, folded in ((0, top + bottom), (1, top - bottom)):
        p, m = fold_columns(mm(down[flip, parity], folded))
        plus[parity * half : (parity + 1) * half] = p
        minus[parity * half : (parity + 1) * half] = m


def row_pass_turned(field, down, flip, plus, minus):
    half = plus.shape[1]
    left, right = field[:, :half], field[:, half:]
    for parity, folded in ((0, left + right), (1, left - right)):
        p, m = fold_columns(mm(down[flip, parity], folded, NT))
        plus[parity * half : (parity + 1) * half] = p
        minus[parity * half : (parity + 1) * half] = m


def column_pass(plus, minus, across, flip, store, store_extra):
    half = plus.shape[1]
    quarter = half // 2
    for col, folded in ((0, plus), (1, minus)):
        table = across[flip, col]
        for row in (0, 1):
            both = mm(folded[row * half : (row + 1) * half], table)
            ea, fa = both[:quarter, :half], both[:quarter, half:]
            eb, fb = both[quarter:, :half], both[quarter:, half:]
            if row == 0:
                store_extra(col, eb[:8], -fb[:8])
                first = lax.broadcasted_iota(jnp.int32, eb.shape, 0) == 0
                eb = jnp.where(first, 0.0, eb)
                fb = jnp.where(first, 0.0, fb)
            store(row, col, ea + fb, eb - fa)


def inverse(packed, back, back_flip, up, up_index, middle):
    half = packed.shape[1] // 2
    quarter = half // 2
    for row in (0, 1):
        rows = packed[row * half : (row + 1) * half]
        parts = []
        for col in (0, 1):
            both = mm(rows[:, col * half : (col + 1) * half], back[back_flip, col])
            ea, fa = both[:quarter, :half], both[:quarter, half:]
            eb, fb = both[quarter:, :half], both[quarter:, half:]
            parts.append((ea - fb, eb + fa))
        (re, ie), (ro, io) = parts
        base = row * half
        middle[base : base + quarter, :half] = (re + ro).astype(BF)
        middle[base : base + quarter, half:] = (re - ro).astype(BF)
        middle[base + quarter : base + half, :half] = (ie + io).astype(BF)
        middle[base + quarter : base + half, half:] = (ie - io).astype(BF)
    even = mm(up_index(up, 0), middle[:half])
    odd = mm(up_index(up, 1), middle[half:])
    return even + odd, even - odd


def blocks(half):
    quarter = half // 2
    for row in (0, 1):
        for col in (0, 1):
            real = (slice(row * half, row * half + quarter), slice(col * half, (col + 1) * half))
            imag = (slice(row * half + quarter, (row + 1) * half), real[1])
            yield row, col, real, imag


def merge_row(real, imag, extra_real, extra_imag):
    pad = jnp.zeros((real.shape[0] - 8, real.shape[1]), F32)
    first = lax.broadcasted_iota(jnp.int32, extra_real.shape, 0) == 0
    extra_real = jnp.concatenate([jnp.where(first, extra_real, 0.0), pad], 0)
    extra_imag = jnp.concatenate([jnp.where(first, extra_imag, 0.0), pad], 0)
    return real - extra_imag, imag + extra_real


def members_of(near):
    member = lax.axis_index("sweep")
    return member // near, member % near


def map_kernel(
    offsets, turns, tiles, sweep, cots, down, across, back, up_sent,
    outgoing, spec, spec_extra, *rest
):
    near = up_sent.shape[1]
    sent, rest = rest[:near], rest[near:]
    plus, minus, swept, swept_extra, total, total_extra, packed, middle = rest[:8]
    staged, in_sems, out_sems = rest[8:]
    q = pl.program_id(0)
    rounds = outgoing.shape[1]
    side = sweep.shape[1]
    half = side // 2
    quarter = half // 2
    moves = pick(offsets, tiles, outgoing, staged, in_sems, out_sems, side // tiles.shape[1])

    @pl.when(q == 0)
    def _():
        for here, load, _ in moves:
            pl.when(here)(load.start)

    hypotheses = cots.shape[1]

    flips = []
    for r in range(hypotheses):
        turn = turns[q, 0, r]
        flip_rows = ((turn == 1) | (turn == 2)).astype(jnp.int32)
        flips.append((turn >= 2).astype(jnp.int32))

        @pl.when(turn % 2 == 0)
        def _():
            row_pass((sweep[0, :half], sweep[0, half:]), down, flip_rows, plus.at[r], minus.at[r])

        @pl.when(turn % 2 == 1)
        def _():
            row_pass_turned(sweep.at[0], down, flip_rows, plus.at[r], minus.at[r])

    for r in range(hypotheses):
        cot = hypotheses + r

        def keep(row, col, real, imag):
            rows = slice(row * quarter, (row + 1) * quarter)
            swept[r, 0, rows, col * half : (col + 1) * half] = real
            swept[r, 1, rows, col * half : (col + 1) * half] = imag

        def keep_extra(col, real, imag):
            swept_extra[r, 0, :, col * half : (col + 1) * half] = real
            swept_extra[r, 1, :, col * half : (col + 1) * half] = imag

        column_pass(plus.at[r], minus.at[r], across, flips[r], keep, keep_extra)
        row_pass((cots[0, r, :half], cots[0, r, half:]), down, 0, plus.at[cot], minus.at[cot])

        def meet(row, col, real, imag):
            base = row * half
            cols = slice(col * half, (col + 1) * half)
            rows = slice(row * quarter, (row + 1) * quarter)
            spec[0, r, base : base + quarter, cols] = real.astype(BF)
            spec[0, r, base + quarter : base + half, cols] = imag.astype(BF)
            sr, si = swept[r, 0, rows, cols], swept[r, 1, rows, cols]
            tr, ti = real * sr - imag * si, real * si + imag * sr
            if r > 0:
                tr, ti = total[0, rows, cols] + tr, total[1, rows, cols] + ti
            if r < hypotheses - 1:
                total[0, rows, cols] = tr
                total[1, rows, cols] = ti
            else:
                if row == 0:
                    tr, ti = merge_row(tr, ti, total_extra[0, :, cols], total_extra[1, :, cols])
                packed[base : base + quarter, cols] = tr.astype(BF)
                packed[base + quarter : base + half, cols] = ti.astype(BF)

        def meet_extra(col, real, imag):
            cols = slice(col * half, (col + 1) * half)
            spec_extra[0, r, 0, :, cols] = real
            spec_extra[0, r, 1, :, cols] = imag
            sr, si = swept_extra[r, 0, :, cols], swept_extra[r, 1, :, cols]
            tr, ti = real * sr - imag * si, real * si + imag * sr
            if r > 0:
                tr, ti = total_extra[0, :, cols] + tr, total_extra[1, :, cols] + ti
            total_extra[0, :, cols] = tr
            total_extra[1, :, cols] = ti

        column_pass(plus.at[cot], minus.at[cot], across, 0, meet, meet_extra)

    _, own = members_of(near)
    ahead = [(own + shift) % near for shift in range(near)]

    def up_index(table, parity):
        return jnp.concatenate([table[parity, y] for y in ahead], 0)

    top, bottom = inverse(packed, back, 0, up_sent, up_index, middle)
    top, bottom = top.astype(BF), bottom.astype(BF)
    rows = half // near
    for shift in range(near):
        sent[shift][0, :rows] = top[shift * rows : (shift + 1) * rows]
        sent[shift][0, rows:] = bottom[shift * rows : (shift + 1) * rows]

    @pl.when(q == 0)
    def _():
        for here, load, store in moves:

            @pl.when(here)
            def _():
                load.wait()
                store.start()

    @pl.when(q == rounds - 1)
    def _():
        for here, _, store in moves:
            pl.when(here)(store.wait)


def sweep_kernel(parts, offsets, turns, *refs):
    quarters, refs = refs[:parts], refs[parts:]
    spec, spec_extra, down, across, back, up, out = refs[:7]
    field, plus, minus, window, window_extra, packed, middle, total = refs[7:]
    q = pl.program_id(0)
    side = out.shape[2]
    half = side // 2
    quarter = half // 2
    span, rows_kept = quarters[0].shape[1:3]
    own_part, _ = members_of(parts)
    for shift in range(parts):
        part = (own_part - shift + parts) % parts
        for k in range(span):
            at = pl.multiple_of((parts * k + part) * rows_kept, rows_kept)
            field[pl.ds(at, rows_kept), :] = quarters[shift][0, k]
    row_pass((field[:half], field[half:]), down, 0, plus, minus)

    def keep(row, col, real, imag):
        rows = slice(row * quarter, (row + 1) * quarter)
        window[0, rows, col * half : (col + 1) * half] = real
        window[1, rows, col * half : (col + 1) * half] = imag

    def keep_extra(col, real, imag):
        window_extra[0, :, col * half : (col + 1) * half] = real
        window_extra[1, :, col * half : (col + 1) * half] = imag

    column_pass(plus, minus, across, 0, keep, keep_extra)
    total[...] = jnp.zeros_like(total)

    for r in range(spec.shape[1]):
        turn = turns[q, 0, r]
        flip_rows = ((turn == 1) | (turn == 2)).astype(jnp.int32)
        flip_cols = (turn >= 2).astype(jnp.int32)
        for row, col, real, imag in blocks(half):
            rows, cols = slice(row * quarter, (row + 1) * quarter), real[1]
            gr, gi = spec[(0, r) + real].astype(F32), spec[(0, r) + imag].astype(F32)
            wr, wi = window[0, rows, cols], window[1, rows, cols]
            br, bi = gr * wr + gi * wi, gr * wi - gi * wr
            if row == 0:
                gr, gi = spec_extra[0, r, 0, :, cols], spec_extra[0, r, 1, :, cols]
                wr, wi = window_extra[0, :, cols], window_extra[1, :, cols]
                br, bi = merge_row(br, bi, gr * wr + gi * wi, gr * wi - gi * wr)
            packed[(r,) + real] = br.astype(BF)
            packed[(r,) + imag] = bi.astype(BF)
        top, bottom = inverse(
            packed.at[r], back, flip_cols, up, lambda u, parity: u[flip_rows, parity], middle.at[r]
        )
        total[turn % 2, :half] += top
        total[turn % 2, half:] += bottom
    out[0, 0] = total[0] + total[1].T


def held_tile(offsets, q, i, span):
    groups = lax.axis_size("tile")
    step = (lax.axis_index("tile") - offsets[q, i] + groups * (groups * span)) % groups
    held = step < span
    return held, jnp.where(held, (offsets[q, i] + step) // groups, 0)


def pick(offsets, tiles, out, staged, in_sems, out_sems, span):
    groups, rounds, rows, _ = out.shape
    part, _ = members_of(tiles.shape[1] // rows)
    first = pl.multiple_of(part * rows, rows)
    moves = []
    for i in range(groups):
        for q in range(rounds):
            here, index = held_tile(offsets, q, i, span)
            load = pltpu.make_async_copy(
                tiles.at[index, pl.ds(first, rows)], staged.at[i, q], in_sems.at[i, q]
            )
            store = pltpu.make_async_copy(staged.at[i, q], out.at[i, q], out_sems.at[i, q])
            moves.append((here, load, store))
    return moves


def choose_kernel(offsets, incoming, mine, out, held):
    rounds, span = out.shape[:2]
    own = lax.axis_index("tile")
    for q in range(rounds):
        for k in range(span):
            out[q, k] = incoming[(offsets[q, own] + k) % incoming.shape[0], q]
    held[...] = mine[...]


def near_kernel(offsets, *refs):
    landed, out, scratch = refs[:-2], refs[-2], refs[-1]
    groups = out.shape[0]
    rounds, span, far, share, side = scratch.shape
    summed = landed[0][...].astype(F32)
    for block in landed[1:]:
        summed += block[...].astype(F32)
    scratch[...] = summed.reshape(rounds, span, far, share, side)
    own = lax.axis_index("tile")
    for i in range(groups):
        parts = []
        for q in range(rounds):
            k = (i - offsets[q, own] + groups * (groups * span)) % groups
            part = scratch[q, jnp.minimum(k, span - 1)]
            parts.append(jnp.where(k < span, part, 0.0))
        out[i] = jnp.concatenate(parts, 1).astype(BF)


def gather_kernel(span, offsets, incoming, out):
    rounds, groups = offsets.shape
    share = out.shape[1]
    out[...] = jnp.zeros_like(out)
    for i in range(groups):
        rows = jnp.sum(incoming[i].astype(F32), 0)
        for q in range(rounds):
            held, index = held_tile(offsets, q, i, span)
            out[index] += jnp.where(held, rows[q * share : (q + 1) * share], 0.0)


def full(shape):
    return pl.BlockSpec(shape, lambda *_: (0,) * len(shape))


SMEM = pl.BlockSpec(memory_space=pltpu.SMEM)
VMEM = pl.BlockSpec(memory_space=pltpu.VMEM)
ANY = pl.BlockSpec(memory_space=pl.ANY)
SMALL = pltpu.CompilerParams(vmem_limit_bytes=12 * 1024 * 1024)
LARGE = pltpu.CompilerParams(vmem_limit_bytes=60 * 1024 * 1024)


def shape(dims, dtype):
    return jax.ShapeDtypeStruct(dims, dtype)


def per_round(dims):
    return pl.BlockSpec((1,) + dims, lambda q: (q,) + (0,) * len(dims))


def shards(map_tiles, sweeps, cotangents, offsets, turn_counts):
    groups = lax.axis_size("tile")
    members = lax.axis_size("sweep")
    tile_rows, side = map_tiles.shape[1:]
    rounds = sweeps.shape[0]
    hypotheses = cotangents.shape[2]
    half = side // 2
    span = side // tile_rows
    share = tile_rows // members
    near = 4
    far = members // near
    sweeps = sweeps[:, 0]
    cotangents = cotangents[:, 0]

    order = (
        np.arange(half).reshape(span // 2, far, near, share).transpose(2, 0, 1, 3).reshape(-1)
    )
    down, across, back, up, up_sent = make_tables(side, order, near)

    part_rows = tile_rows // far
    unit = 2 * side**3
    outgoing, spec, spec_extra, *sent = pl.pallas_call(
        map_kernel,
        grid=(rounds,),
        out_shape=[
            shape((groups, rounds, part_rows, side), BF),
            shape((rounds, hypotheses, side, side), BF),
            shape((rounds, hypotheses, 2, 8, side), F32),
            *[shape((rounds, side // near, side), BF)] * near,
        ],
        in_specs=[
            SMEM,
            SMEM,
            ANY,
            per_round((side, side)),
            per_round((hypotheses, side, side)),
            full(down.shape),
            full(across.shape),
            full((1,) + back.shape[1:]),
            full(up_sent.shape),
        ],
        out_specs=[
            ANY,
            per_round((hypotheses, side, side)),
            per_round((hypotheses, 2, 8, side)),
            *[per_round((side // near, side))] * near,
        ],
        scratch_shapes=[
            pltpu.VMEM((2 * hypotheses, side, half), BF),
            pltpu.VMEM((2 * hypotheses, side, half), BF),
            pltpu.VMEM((hypotheses, 2, half, side), F32),
            pltpu.VMEM((hypotheses, 2, 8, side), F32),
            pltpu.VMEM((2, half, side), F32),
            pltpu.VMEM((2, 8, side), F32),
            pltpu.VMEM((side, side), BF),
            pltpu.VMEM((side, side), BF),
            pltpu.VMEM((groups, rounds, part_rows, side), BF),
            pltpu.SemaphoreType.DMA((groups, rounds)),
            pltpu.SemaphoreType.DMA((groups, rounds)),
        ],
        compiler_params=LARGE,
        cost_estimate=pl.CostEstimate(
            flops=int(8 * rounds * unit), bytes_accessed=8 * 1024 * 1024, transcendentals=0
        ),
        name="map_terms",
    )(offsets, turn_counts, map_tiles, sweeps, cotangents, down, across, back, up_sent)
    incoming = lax.all_to_all(outgoing, "tile", split_axis=0, concat_axis=0, tiled=True)
    kept, held = pl.pallas_call(
        choose_kernel,
        out_shape=[shape((rounds, span, part_rows, side), BF), shape(sent[0].shape, BF)],
        in_specs=[SMEM, VMEM, VMEM],
        out_specs=[VMEM] * 2,
        compiler_params=SMALL,
        name="choose",
    )(offsets, incoming, sent[0])
    quarters = [kept] + [
        lax.ppermute(kept, "sweep", [(m, (m + shift * near) % members) for m in range(members)])
        for shift in range(1, far)
    ]
    landed = [held]
    for shift in range(1, near):
        pairs = [(m, m // near * near + (m + shift) % near) for m in range(members)]
        landed.append(lax.ppermute(sent[shift], "sweep", pairs))

    placed = pl.pallas_call(
        near_kernel,
        out_shape=shape((groups, far, rounds * share, side), BF),
        in_specs=[SMEM] + [VMEM] * near,
        out_specs=VMEM,
        scratch_shapes=[pltpu.VMEM((rounds, span, far, share, side), F32)],
        compiler_params=SMALL,
        name="near_sum",
    )(offsets, *landed)
    index_groups = [
        [t * members + f * near + y for t in range(groups) for f in range(far)] for y in range(near)
    ]
    owned = lax.all_to_all(
        placed.reshape(groups * far, rounds * share, side),
        ("tile", "sweep"),
        split_axis=0,
        concat_axis=0,
        tiled=True,
        axis_index_groups=index_groups,
    )
    grad_map = pl.pallas_call(
        partial(gather_kernel, span),
        out_shape=shape((map_tiles.shape[0], share, side), F32),
        in_specs=[SMEM, VMEM],
        out_specs=VMEM,
        compiler_params=SMALL,
        name="gather",
    )(offsets, owned.reshape(groups, far, rounds * share, side))

    grad_sweeps = pl.pallas_call(
        partial(sweep_kernel, far),
        grid=(rounds,),
        out_shape=shape((rounds, 1, side, side), F32),
        in_specs=[
            SMEM,
            SMEM,
            *[per_round((span, part_rows, side))] * far,
            per_round((hypotheses, side, side)),
            per_round((hypotheses, 2, 8, side)),
            full((1,) + down.shape[1:]),
            full((1,) + across.shape[1:]),
            full(back.shape),
            full(up.shape),
        ],
        out_specs=per_round((1, side, side)),
        scratch_shapes=[
            pltpu.VMEM((side, side), BF),
            pltpu.VMEM((side, half), BF),
            pltpu.VMEM((side, half), BF),
            pltpu.VMEM((2, half, side), F32),
            pltpu.VMEM((2, 8, side), F32),
            pltpu.VMEM((hypotheses, side, side), BF),
            pltpu.VMEM((hypotheses, side, side), BF),
            pltpu.VMEM((2, side, side), F32),
        ],
        compiler_params=LARGE,
        cost_estimate=pl.CostEstimate(
            flops=int(5 * rounds * unit), bytes_accessed=8 * 1024 * 1024, transcendentals=0
        ),
        name="sweep_terms",
    )(offsets, turn_counts, *quarters, spec, spec_extra, down, across, back, up)
    return grad_map, grad_sweeps


def solution(mesh):
    in_specs = (
        P("tile", None, None),
        P(None, ("tile", "sweep"), None, None),
        P(None, ("tile", "sweep"), None, None, None),
        P(),
        P(None, ("tile", "sweep"), None),
    )
    out_specs = (P("tile", "sweep", None), P(None, ("tile", "sweep"), None, None))
    return jax.shard_map(shards, mesh=mesh, in_specs=in_specs, out_specs=out_specs, check_vma=False)
```
